32 devices in a mesh: seg: 4 (over y, core), band: 8 (over z, x).
Axes of the slice: x: 2, y: 2, z: 4, core: 2. Of those that a mesh axis runs over, the one named last changes fastest.
Arguments:
- sft: bfloat16 [8, 2, 2, 2048], P('seg', None, None, 'band'), may hold values from -6 to 6
- doppler: float32 [8, 512], P('seg'), may hold values from -16 to 16
- antenna: float32 [8, 2, 2, 512], P('seg'), may hold values from -1 to 1
- coarse_index: int32 [8, 128], P('seg'), may hold values from 0 to 511
- freq_offset: int32 [8, 128], P('seg'), may hold values from -32 to 32
- wing_width: int32 [8], replicated, may hold values from 8 to 32
Outputs:
- fstat: float32 [128, 2048], P('seg', 'band')
The draws below stay inside these ranges and needn't reach their ends.
All inputs are finite; a program needn't handle non-finite values.
Results may differ from the reference program's by a relative error of at most 0.00088.
Values may be sent and summed in bfloat16 or wider, within the bound.
A program may use at most 64 MiB of HBM per device.

```python
import math
import jax
import jax.numpy as jnp
from jax import lax

DET = 2
WMAX = 32
OMAX = 32
BINS_DEV = 256
COARSE = 512
SEGMENTS = 8
BINS = 2048
FINE = 128
N_BAND = 8


def touch_ends(array, key, low, largest):
    dims = array.shape
    spot = [jax.random.randint(jax.random.fold_in(key, axis), (), 0, dims[axis]) for axis in range(len(dims))]
    array = array.at[tuple(spot)].set(low)
    longest = dims.index(max(dims))
    spot[longest] = (spot[longest] + 1) % dims[longest]
    return array.at[tuple(spot)].set(largest)


def block_levels(stream_key, shape, shards, least, high):
    def one(axis_at, parts):
        heights = jax.random.uniform(jax.random.fold_in(jax.random.fold_in(stream_key, 6), axis_at), (parts,), jnp.float32, least / len(shards), high / len(shards))
        return jnp.repeat(jnp.exp(heights), shape[axis_at] // parts).reshape((-1,) + (1,) * (len(shape) - axis_at - 1))

    loudness = one(*shards[0])
    for cut in shards[1:]:
        loudness = loudness * one(*cut)
    return loudness


def normal_values(stream_key, dims, scale, limit, pieces=(), held_as=jnp.bfloat16):
    entries = jax.random.normal(stream_key, dims, jnp.float32) * scale
    if len(pieces) > 0:
        entries = block_levels(stream_key, dims, pieces, -0.22, 0.18) * entries
    return jnp.clip(entries, min=-limit, max=limit).astype(held_as)


def setup_inputs(seed: int = 0) -> dict:
    key_of = jax.random.split(jax.random.key(seed), 7)
    return {
        "sft": normal_values(key_of[0], (SEGMENTS, DET, 2, BINS), 1.0, 6.0, ((0, 4), (3, 8))),
        "doppler": jnp.clip(jax.random.uniform(key_of[1], (SEGMENTS, COARSE), jnp.float32, -16.0, 16.0) * block_levels(key_of[1], (SEGMENTS, COARSE), ((0, 4),), -0.4, 0.0), -16.0, 16.0),
        "antenna": jnp.clip(jax.random.uniform(key_of[2], (SEGMENTS, 2, DET, COARSE), jnp.float32, -1.0, 1.0) * block_levels(key_of[2], (SEGMENTS, 2, DET, COARSE), ((0, 4),), -0.4, 0.0), -1.0, 1.0),
        "coarse_index": touch_ends(jax.random.randint(key_of[3], (SEGMENTS, FINE), 0, COARSE), jax.random.fold_in(key_of[3], 1), 0, COARSE - 1).astype(jnp.int32),
        "freq_offset": touch_ends(jax.random.randint(key_of[4], (SEGMENTS, FINE), 0 - OMAX, OMAX + 1), jax.random.fold_in(key_of[4], 1), 0 - OMAX, OMAX).astype(jnp.int32),
        "wing_width": touch_ends(jax.random.randint(key_of[5], (N_BAND,), WMAX // 4, WMAX + 1), jax.random.fold_in(key_of[5], 1), WMAX // 4, WMAX).astype(jnp.int32),
    }


def kernel_block(shifts, weights):
    tap_pos = jnp.arange(2 * WMAX).astype(jnp.float32) - WMAX
    offsets = tap_pos[None, None, :] - shifts[:, :, None]
    envelope = jnp.sinc(offsets)
    real_part = envelope * jnp.cos(jnp.pi * offsets)
    imag_part = -envelope * jnp.sin(jnp.pi * offsets)
    from_real = jnp.stack([real_part, imag_part], -1)
    from_imag = jnp.stack([-imag_part, real_part], -1)
    stacked = jnp.transpose(jnp.stack([from_real, from_imag], 1), (0, 1, 3, 2, 4))
    antenna_t = jnp.transpose(weights, (0, 2, 3, 1))
    product = antenna_t[:, :, None, None, :, :, None] * stacked[:, None, :, :, :, None, :]
    count_seg = shifts.shape[0]
    return product.astype(jnp.bfloat16).reshape(count_seg, -1, shifts.shape[1] * 4)


def coarse_stat(padded, doppler, antenna, wing_width, first_bin, bin_count, band_bins):
    segs_here = padded.shape[0]
    tap_count = 2 * WMAX
    unfolded = jnp.stack([padded[:, :, :, column:column + bin_count] for column in range(tap_count)], axis=3)
    global_bin = first_bin + jnp.arange(bin_count).astype(jnp.int32)
    subband = global_bin // band_bins
    member = subband[:, None] == jnp.arange(wing_width.shape[0]).astype(jnp.int32)[None, :]
    wing_reach = jnp.sum(jnp.where(member, wing_width[None, :], 0), axis=1)
    tap_index = jnp.arange(tap_count).astype(jnp.int32) - WMAX
    inside = (tap_index[:, None] >= -wing_reach[None, :]) & (tap_index[:, None] < wing_reach[None, :])
    unfolded = unfolded * inside.astype(jnp.bfloat16)
    unfolded = unfolded.reshape(segs_here, -1, bin_count).astype(jnp.float32)
    coarse_count = doppler.shape[1]
    block_size = math.gcd(coarse_count, 256)
    blocks = coarse_count // block_size
    shift_blocks = jnp.moveaxis(doppler.reshape(segs_here, blocks, block_size), 1, 0)
    weight_blocks = jnp.moveaxis(antenna.reshape(segs_here, 2, antenna.shape[2], blocks, block_size), 3, 0)

    def one_block(block_args):
        kernel = kernel_block(block_args[0], block_args[1]).astype(jnp.float32)
        amplitude = jnp.einsum("skf,skn->snf", unfolded, kernel)
        amplitude = amplitude.reshape(segs_here, block_size, 4, bin_count)
        return 0.25 * jnp.sum(amplitude * amplitude, axis=2)

    result = lax.map(one_block, (shift_blocks, weight_blocks))
    return jnp.transpose(result, (1, 0, 2, 3)).reshape(segs_here, coarse_count, bin_count)


def reference(sft, doppler, antenna, coarse_index, freq_offset, wing_width):
    all_bins = sft.shape[3]

    def one_segment(partial_sum, inputs):
        segment_sft, shifts, weights, indices, offsets = inputs
        padded = jnp.pad(segment_sft, ((0, 0), (0, 0), (WMAX, WMAX)))[None]
        coarse = coarse_stat(padded, shifts[None], weights[None], wing_width, 0, all_bins, BINS_DEV)[0]
        coarse = jnp.pad(coarse, ((0, 0), (OMAX, OMAX)))
        picked = jnp.take(coarse, indices, axis=0)
        moved = jax.vmap(lambda row_data, shift_bins: lax.dynamic_slice_in_dim(row_data, (shift_bins + OMAX).astype(jnp.int32), all_bins))(picked, offsets)
        return partial_sum + moved, None

    initial = jnp.zeros((coarse_index.shape[1], all_bins), jnp.float32)
    total, unused = lax.scan(one_segment, initial, (sft, doppler, antenna, coarse_index, freq_offset))
    return total / SEGMENTS
```

```python
import functools
import math

import jax
import jax.numpy as jnp
from jax import lax
from jax.experimental import pallas as pl
from jax.experimental.pallas import tpu as pltpu
from jax.sharding import PartitionSpec as P

WMAX = 32
OMAX = 32
TAPS = 2 * WMAX
LANES = 128
ROWS = 8
MESH = pl.DeviceIdType.MESH


def half_turn(x):
    rest = x - jnp.round(x)
    angle = rest * math.pi
    square = angle * angle
    sine = jnp.zeros_like(x)
    cosine = jnp.zeros_like(x)
    for power in range(7, -1, -1):
        sign = -1.0 if power % 2 else 1.0
        cosine = cosine * square + sign / math.factorial(2 * power)
        sine = sine * square + sign / math.factorial(2 * power + 1)
    return sine * angle, cosine


def gathered_rows(rows, indices):
    first = rows.astype(jnp.bfloat16).astype(jnp.float32)
    rest = rows - first
    second = rest.astype(jnp.bfloat16).astype(jnp.float32)
    third = rest - second
    parts = jnp.concatenate([first, second, third, jnp.zeros_like(first)], axis=0)
    places = lax.broadcasted_iota(jnp.int32, (rows.shape[1], indices.shape[1]), 0)
    chosen = jnp.where(places == indices, 1.0, 0.0).astype(jnp.bfloat16)
    picked = jnp.dot(parts.astype(jnp.bfloat16), chosen, preferred_element_type=jnp.float32)
    count = rows.shape[0]
    return picked[:count] + picked[count : 2 * count] + picked[2 * count : 3 * count]


def kernel(
    n_seg,
    n_band,
    scale,
    sft_ref,
    doppler_ref,
    antenna_ref,
    index_ref,
    offset_ref,
    wing_ref,
    out_ref,
    x_ref,
    edge_ref,
    param_ref,
    fine_ref,
    part_ref,
    recv_ref,
    edge_send,
    edge_recv,
    part_send,
    part_recv,
):
    seg = lax.axis_index("seg")
    band = lax.axis_index("band")
    segs_here, dets, _, bins = sft_ref.shape
    fine = index_ref.shape[1]
    own = fine // n_seg
    lines = 2 * dets
    up = lax.rem(band + 1, n_band)
    down = lax.rem(band + n_band - 1, n_band)

    barrier = pltpu.get_barrier_semaphore()
    for neighbour in (up, down):
        pl.semaphore_signal(barrier, inc=1, device_id={"band": neighbour}, device_id_type=MESH)
    for step in range(1, n_seg):
        pl.semaphore_signal(
            barrier,
            inc=1,
            device_id={"seg": lax.rem(seg + step, n_seg)},
            device_id_type=MESH,
        )

    for s in range(segs_here):
        for d in range(dets):
            first = s * lines + 2 * d
            x_ref[first : first + 2, :] = sft_ref[s, d].astype(jnp.float32)
    pl.semaphore_wait(barrier, n_seg + 1)

    edges = []
    for side, (neighbour, start) in enumerate(((up, bins - LANES), (down, 0))):
        edges.append(
            pltpu.make_async_remote_copy(
                src_ref=x_ref.at[:, pl.ds(start, LANES)],
                dst_ref=edge_ref.at[side],
                send_sem=edge_send.at[side],
                recv_sem=edge_recv.at[side],
                device_id={"band": neighbour},
                device_id_type=MESH,
            )
        )
        edges[-1].start()

    param_ref[...] = jnp.zeros_like(param_ref)
    fine_ref[...] = jnp.zeros_like(fine_ref)
    for s in range(segs_here):
        param_ref[ROWS * s : ROWS * s + 1, :] = doppler_ref[s : s + 1, :]
        for q in range(2):
            first = ROWS * s + 1 + dets * q
            param_ref[first : first + dets, :] = antenna_ref[s, q]
    for s in range(segs_here):
        rows = gathered_rows(param_ref[ROWS * s : ROWS * (s + 1), :], index_ref[s : s + 1, :])
        fine_ref[ROWS * s : ROWS * (s + 1), :] = rows
        sine, cosine = half_turn(rows[0:1])
        fine_ref[ROWS * s + 5 : ROWS * s + 6, :] = offset_ref[s : s + 1, :].astype(jnp.float32)
        fine_ref[ROWS * s + 6 : ROWS * s + 7, :] = sine
        fine_ref[ROWS * s + 7 : ROWS * s + 8, :] = cosine
    columns = jnp.transpose(fine_ref[...])

    lane = lax.broadcasted_iota(jnp.int32, (fine, 2 * TAPS), 1)
    from_real = lane < TAPS
    tap = (WMAX - 1 - lax.rem(lane, TAPS)).astype(jnp.float32)
    kernels = []
    for s in range(segs_here):
        column = lambda row: columns[:, ROWS * s + row : ROWS * s + row + 1]
        u = tap - column(0)
        centre = u == 0.0
        envelope = jnp.where(
            centre, 1.0, -column(6) / jnp.where(centre, 1.0, math.pi * u)
        )
        real_part = envelope * column(7)
        imag_part = envelope * column(6)
        to_real = jnp.where(from_real, real_part, -imag_part)
        to_imag = jnp.where(from_real, imag_part, real_part)
        blocks = []
        for q in range(2):
            for shape in (to_real, to_imag):
                pieces = [column(1 + dets * q + d) * shape for d in range(dets)]
                blocks.append(jnp.concatenate(pieces, axis=1))
        kernels.append(jnp.concatenate(blocks, axis=0).astype(jnp.bfloat16))

    width = bins + 2 * (WMAX + OMAX)
    wing_low = jnp.where(band > 0, wing_ref[jnp.maximum(band - 1, 0)], 0)
    wing_mid = wing_ref[band]
    wing_high = jnp.where(band < n_band - 1, wing_ref[jnp.minimum(band + 1, n_band - 1)], 0)
    position = lax.broadcasted_iota(jnp.int32, (TAPS, width), 1)
    reach = jnp.where(
        position < OMAX, wing_low, jnp.where(position < OMAX + bins, wing_mid, wing_high)
    )
    tap_here = WMAX - 1 - lax.broadcasted_iota(jnp.int32, (TAPS, width), 0)
    inside = (tap_here >= -reach) & (tap_here < reach)

    for edge in edges:
        edge.wait()
    low = jnp.where(band > 0, edge_ref[0], 0.0)
    high = jnp.where(band < n_band - 1, edge_ref[1], 0.0)
    padded = jnp.concatenate([low, x_ref[...], high], axis=1)
    margin = LANES - WMAX - OMAX
    padded = pltpu.roll(padded, padded.shape[1] - margin, 1)[:, :width]

    total = None
    for s in range(segs_here):
        unfolded = []
        for line in range(s * lines, (s + 1) * lines):
            spread = jnp.broadcast_to(padded[line : line + 1, :], (TAPS, width))
            spread = pltpu.roll(spread, width - TAPS + 1, 1, stride=1, stride_axis=0)
            unfolded.append(jnp.where(inside, spread, 0.0))
        unfolded = jnp.concatenate(unfolded, axis=0).astype(jnp.bfloat16)
        amplitude = jnp.dot(kernels[s], unfolded, preferred_element_type=jnp.float32)
        power = amplitude * amplitude
        coarse = (power[:fine] + power[fine : 2 * fine]) + (
            power[2 * fine : 3 * fine] + power[3 * fine :]
        )
        shift = columns[:, ROWS * s + 5 : ROWS * s + 6].astype(jnp.int32) + OMAX
        for bit in range((2 * OMAX).bit_length()):
            moved = pltpu.roll(coarse, width - (1 << bit), 1)
            coarse = jnp.where((shift & (1 << bit)) != 0, moved, coarse)
        total = coarse[:, :bins] if total is None else total + coarse[:, :bins]
    part_ref[...] = total * scale

    sends = []
    for step in range(1, n_seg):
        peer = lax.rem(seg + step, n_seg)
        sends.append(
            pltpu.make_async_remote_copy(
                src_ref=part_ref.at[pl.ds(pl.multiple_of(peer * own, own), own)],
                dst_ref=recv_ref.at[step - 1],
                send_sem=part_send.at[step - 1],
                recv_sem=part_recv.at[step - 1],
                device_id={"seg": peer},
                device_id_type=MESH,
            )
        )
        sends[-1].start()
    result = part_ref[pl.ds(pl.multiple_of(seg * own, own), own), :]
    for step in range(1, n_seg):
        sends[step - 1].wait_recv()
        result = result + recv_ref[step - 1]
    out_ref[...] = result
    for send in sends:
        send.wait_send()


def solution(mesh):
    n_seg = mesh.shape["seg"]
    n_band = mesh.shape["band"]
    placed = (
        P("seg", None, None, "band"),
        P("seg", None),
        P("seg", None, None, None),
        P("seg", None),
        P("seg", None),
        P(),
    )

    def per_device(sft, doppler, antenna, coarse_index, freq_offset, wing_width):
        segs_here, dets, _, bins = sft.shape
        fine = coarse_index.shape[1]
        own = fine // n_seg
        lines = segs_here * dets * 2
        vmem = pl.BlockSpec(memory_space=pltpu.VMEM)
        smem = pl.BlockSpec(memory_space=pltpu.SMEM)
        return pl.pallas_call(
            functools.partial(kernel, n_seg, n_band, 0.25 / (segs_here * n_seg)),
            out_shape=jax.ShapeDtypeStruct((own, bins), jnp.float32),
            in_specs=[vmem] * 5 + [smem],
            out_specs=vmem,
            scratch_shapes=[
                pltpu.VMEM((lines, bins), jnp.float32),
                pltpu.VMEM((2, lines, LANES), jnp.float32),
                pltpu.VMEM((ROWS * segs_here, doppler.shape[1]), jnp.float32),
                pltpu.VMEM((LANES, fine), jnp.float32),
                pltpu.VMEM((fine, bins), jnp.float32),
                pltpu.VMEM((n_seg - 1, own, bins), jnp.float32),
                pltpu.SemaphoreType.DMA((2,)),
                pltpu.SemaphoreType.DMA((2,)),
                pltpu.SemaphoreType.DMA((n_seg - 1,)),
                pltpu.SemaphoreType.DMA((n_seg - 1,)),
            ],
            compiler_params=pltpu.CompilerParams(
                collective_id=0, has_side_effects=True, vmem_limit_bytes=40 * 1024 * 1024
            ),
        )(sft, doppler, antenna, coarse_index, freq_offset, wing_width)

    return jax.shard_map(
        per_device, mesh=mesh, in_specs=placed, out_specs=P("seg", "band"), check_vma=False
    )
```

```python
import functools
import math

import jax
import jax.numpy as jnp
from jax import lax
from jax.experimental import pallas as pl
from jax.experimental.pallas import tpu as pltpu
from jax.sharding import PartitionSpec as P

WMAX = 32
OMAX = 32
TAPS = 2 * WMAX
LANES = 128
ROWS = 8
MESH = pl.DeviceIdType.MESH


def half_turn(x):
    rest = x - jnp.round(x)
    angle = rest * math.pi
    square = angle * angle
    sine = jnp.zeros_like(x)
    cosine = jnp.zeros_like(x)
    for power in range(7, -1, -1):
        sign = -1.0 if power % 2 else 1.0
        cosine = cosine * square + sign / math.factorial(2 * power)
        sine = sine * square + sign / math.factorial(2 * power + 1)
    return sine * angle, cosine


def gathered_rows(rows, indices):
    first = rows.astype(jnp.bfloat16).astype(jnp.float32)
    rest = rows - first
    second = rest.astype(jnp.bfloat16).astype(jnp.float32)
    third = rest - second
    parts = jnp.concatenate([first, second, third, jnp.zeros_like(first)], axis=0)
    places = lax.broadcasted_iota(jnp.int32, (rows.shape[1], indices.shape[1]), 0)
    chosen = jnp.where(places == indices, 1.0, 0.0).astype(jnp.bfloat16)
    picked = jnp.dot(parts.astype(jnp.bfloat16), chosen, preferred_element_type=jnp.float32)
    count = rows.shape[0]
    return picked[:count] + picked[count : 2 * count] + picked[2 * count : 3 * count]


def kernel(
    n_seg,
    n_band,
    scale,
    sft_hbm,
    doppler_hbm,
    antenna_hbm,
    index_hbm,
    offset_hbm,
    wing_hbm,
    out_ref,
    sft_ref,
    doppler_ref,
    antenna_ref,
    index_ref,
    offset_ref,
    wing_ref,
    x_ref,
    edge_ref,
    param_ref,
    fine_ref,
    column_ref,
    kernel_ref,
    part_ref,
    recv_ref,
    load_sem,
    edge_send,
    edge_recv,
    part_send,
    part_recv,
):
    seg = lax.axis_index("seg")
    band = lax.axis_index("band")
    segs_here, dets, _, bins = sft_ref.shape
    fine = index_ref.shape[1]
    own = fine // n_seg
    lines = 2 * dets
    has_up = band < n_band - 1
    has_down = band > 0
    up = jnp.minimum(band + 1, n_band - 1)
    down = jnp.maximum(band - 1, 0)

    barrier = pltpu.get_barrier_semaphore()
    for there, neighbour in ((has_up, up), (has_down, down)):

        @pl.when(there)
        def _():
            pl.semaphore_signal(
                barrier, inc=1, device_id={"band": neighbour}, device_id_type=MESH
            )

    for step in range(1, n_seg):
        pl.semaphore_signal(
            barrier,
            inc=1,
            device_id={"seg": lax.rem(seg + step, n_seg)},
            device_id_type=MESH,
        )

    loads = []
    for source, target in (
        (sft_hbm, sft_ref),
        (doppler_hbm, doppler_ref),
        (antenna_hbm, antenna_ref),
        (index_hbm, index_ref),
        (offset_hbm, offset_ref),
        (wing_hbm, wing_ref),
    ):
        loads.append(pltpu.make_async_copy(source, target, load_sem.at[len(loads)]))
        loads[-1].start()
    loads[0].wait()
    for s in range(segs_here):
        for d in range(dets):
            first = s * lines + 2 * d
            x_ref[first : first + 2, :] = sft_ref[s, d].astype(jnp.float32)
    neighbours = n_seg - 1 + has_up.astype(jnp.int32) + has_down.astype(jnp.int32)
    pl.semaphore_wait(barrier, neighbours)

    def edge_copy(side):
        start, neighbour = ((bins - LANES, up), (0, down))[side]
        return pltpu.make_async_remote_copy(
            src_ref=x_ref.at[:, pl.ds(start, LANES)],
            dst_ref=edge_ref.at[side],
            send_sem=edge_send.at[side],
            recv_sem=edge_recv.at[side],
            device_id={"band": neighbour},
            device_id_type=MESH,
        )

    for side, there in enumerate((has_up, has_down)):

        @pl.when(there)
        def _():
            edge_copy(side).start()

    for load in loads[1:]:
        load.wait()
    param_ref[...] = jnp.zeros_like(param_ref)
    fine_ref[...] = jnp.zeros_like(fine_ref)
    for s in range(segs_here):
        param_ref[ROWS * s : ROWS * s + 1, :] = doppler_ref[s : s + 1, :]
        for q in range(2):
            first = ROWS * s + 1 + dets * q
            param_ref[first : first + dets, :] = antenna_ref[s, q]
    for s in range(segs_here):
        rows = gathered_rows(param_ref[ROWS * s : ROWS * (s + 1), :], index_ref[s : s + 1, :])
        fine_ref[ROWS * s : ROWS * (s + 1), :] = rows
        sine, cosine = half_turn(rows[0:1])
        fine_ref[ROWS * s + 5 : ROWS * s + 6, :] = offset_ref[s : s + 1, :].astype(jnp.float32)
        fine_ref[ROWS * s + 6 : ROWS * s + 7, :] = sine
        fine_ref[ROWS * s + 7 : ROWS * s + 8, :] = cosine
    columns = jnp.transpose(fine_ref[...])
    column_ref[...] = columns

    lane = lax.broadcasted_iota(jnp.int32, (fine, 2 * TAPS), 1)
    from_real = lane < TAPS
    tap = (WMAX - 1 - lax.rem(lane, TAPS)).astype(jnp.float32)
    for s in range(segs_here):
        column = lambda row: columns[:, ROWS * s + row : ROWS * s + row + 1]
        u = tap - column(0)
        centre = u == 0.0
        envelope = jnp.where(
            centre, 1.0, -column(6) / jnp.where(centre, 1.0, math.pi * u)
        )
        real_part = envelope * column(7)
        imag_part = envelope * column(6)
        to_real = jnp.where(from_real, real_part, -imag_part)
        to_imag = jnp.where(from_real, imag_part, real_part)
        for q in range(2):
            for part, shape in enumerate((to_real, to_imag)):
                for d in range(dets):
                    piece = column(1 + dets * q + d) * shape
                    kernel_ref[s, 2 * q + part, :, 2 * TAPS * d : 2 * TAPS * (d + 1)] = (
                        piece.astype(jnp.bfloat16)
                    )

    width = bins + 2 * (WMAX + OMAX)
    wing_low = jnp.where(has_down, wing_ref[down], 0)
    wing_mid = wing_ref[band]
    wing_high = jnp.where(has_up, wing_ref[up], 0)
    position = lax.broadcasted_iota(jnp.int32, (TAPS, width), 1)
    reach = jnp.where(
        position < OMAX, wing_low, jnp.where(position < OMAX + bins, wing_mid, wing_high)
    )
    tap_here = WMAX - 1 - lax.broadcasted_iota(jnp.int32, (TAPS, width), 0)
    inside = (tap_here >= -reach) & (tap_here < reach)

    for side, there in enumerate((has_down, has_up)):

        @pl.when(there)
        def _():
            edge_copy(side).wait_recv()

    low = jnp.where(has_down, edge_ref[0], 0.0)
    high = jnp.where(has_up, edge_ref[1], 0.0)
    padded = jnp.concatenate([low, x_ref[...], high], axis=1)
    margin = LANES - WMAX - OMAX
    padded = pltpu.roll(padded, padded.shape[1] - margin, 1)[:, :width]

    transforms = []
    for s in range(segs_here):
        unfolded = []
        for line in range(s * lines, (s + 1) * lines):
            spread = jnp.broadcast_to(padded[line : line + 1, :], (TAPS, width))
            spread = pltpu.roll(spread, width - TAPS + 1, 1, stride=1, stride_axis=0)
            unfolded.append(jnp.where(inside, spread, 0.0))
        transforms.append(jnp.concatenate(unfolded, axis=0).astype(jnp.bfloat16))

    def fine_block(owner):
        rows = pl.ds(pl.multiple_of(owner * own, own), own)
        columns = column_ref[rows, :]
        total = None
        for s in range(segs_here):
            taps = jnp.concatenate([kernel_ref[s, part, rows, :] for part in range(4)], axis=0)
            amplitude = jnp.dot(taps, transforms[s], preferred_element_type=jnp.float32)
            power = amplitude * amplitude
            coarse = (power[:own] + power[own : 2 * own]) + (
                power[2 * own : 3 * own] + power[3 * own :]
            )
            shift = columns[:, ROWS * s + 5 : ROWS * s + 6].astype(jnp.int32) + OMAX
            for bit in range((2 * OMAX).bit_length()):
                moved = pltpu.roll(coarse, width - (1 << bit), 1)
                coarse = jnp.where((shift & (1 << bit)) != 0, moved, coarse)
            total = coarse[:, :bins] if total is None else total + coarse[:, :bins]
        return total * scale

    sends = []
    for step in range(1, n_seg):
        peer = lax.rem(seg + step, n_seg)
        part_ref[step - 1] = fine_block(peer)
        sends.append(
            pltpu.make_async_remote_copy(
                src_ref=part_ref.at[step - 1],
                dst_ref=recv_ref.at[step - 1],
                send_sem=part_send.at[step - 1],
                recv_sem=part_recv.at[step - 1],
                device_id={"seg": peer},
                device_id_type=MESH,
            )
        )
        sends[-1].start()
    result = fine_block(seg)
    for step in range(1, n_seg):
        sends[step - 1].wait_recv()
        result = result + recv_ref[step - 1]
    out_ref[...] = result
    for send in sends:
        send.wait_send()
    for side, there in enumerate((has_up, has_down)):

        @pl.when(there)
        def _():
            edge_copy(side).wait_send()


def solution(mesh):
    n_seg = mesh.shape["seg"]
    n_band = mesh.shape["band"]
    placed = (
        P("seg", None, None, "band"),
        P("seg", None),
        P("seg", None, None, None),
        P("seg", None),
        P("seg", None),
        P(),
    )

    def per_device(sft, doppler, antenna, coarse_index, freq_offset, wing_width):
        segs_here, dets, _, bins = sft.shape
        fine = coarse_index.shape[1]
        own = fine // n_seg
        lines = segs_here * dets * 2
        vmem = pl.BlockSpec(memory_space=pltpu.VMEM)
        hbm = pl.BlockSpec(memory_space=pltpu.HBM)
        return pl.pallas_call(
            functools.partial(kernel, n_seg, n_band, 0.25 / (segs_here * n_seg)),
            out_shape=jax.ShapeDtypeStruct((own, bins), jnp.float32),
            in_specs=[hbm] * 6,
            out_specs=vmem,
            scratch_shapes=[
                pltpu.VMEM(sft.shape, sft.dtype),
                pltpu.VMEM(doppler.shape, doppler.dtype),
                pltpu.VMEM(antenna.shape, antenna.dtype),
                pltpu.VMEM(coarse_index.shape, coarse_index.dtype),
                pltpu.VMEM(freq_offset.shape, freq_offset.dtype),
                pltpu.SMEM(wing_width.shape, wing_width.dtype),
                pltpu.VMEM((lines, bins), jnp.float32),
                pltpu.VMEM((2, lines, LANES), jnp.float32),
                pltpu.VMEM((ROWS * segs_here, doppler.shape[1]), jnp.float32),
                pltpu.VMEM((LANES, fine), jnp.float32),
                pltpu.VMEM((fine, LANES), jnp.float32),
                pltpu.VMEM((segs_here, 4, fine, 2 * TAPS * dets), jnp.bfloat16),
                pltpu.VMEM((n_seg - 1, own, bins), jnp.float32),
                pltpu.VMEM((n_seg - 1, own, bins), jnp.float32),
                pltpu.SemaphoreType.DMA((6,)),
                pltpu.SemaphoreType.DMA((2,)),
                pltpu.SemaphoreType.DMA((2,)),
                pltpu.SemaphoreType.DMA((n_seg - 1,)),
                pltpu.SemaphoreType.DMA((n_seg - 1,)),
            ],
            compiler_params=pltpu.CompilerParams(
                collective_id=0, has_side_effects=True, vmem_limit_bytes=60 * 1024 * 1024
            ),
        )(sft, doppler, antenna, coarse_index, freq_offset, wing_width)

    return jax.shard_map(
        per_device, mesh=mesh, in_specs=placed, out_specs=P("seg", "band"), check_vma=False
    )
```

```python
import functools
import math

import jax
import jax.numpy as jnp
from jax import lax
from jax.experimental import pallas as pl
from jax.experimental.pallas import tpu as pltpu
from jax.sharding import PartitionSpec as P

WMAX = 32
OMAX = 32
TAPS = 2 * WMAX
LANES = 128
ROWS = 8
MESH = pl.DeviceIdType.MESH


def half_turn(x):
    rest = x - jnp.round(x)
    angle = rest * math.pi
    square = angle * angle
    sine = jnp.zeros_like(x)
    cosine = jnp.zeros_like(x)
    for power in range(7, -1, -1):
        sign = -1.0 if power % 2 else 1.0
        cosine = cosine * square + sign / math.factorial(2 * power)
        sine = sine * square + sign / math.factorial(2 * power + 1)
    return sine * angle, cosine


def gathered_rows(rows, indices):
    first = rows.astype(jnp.bfloat16).astype(jnp.float32)
    rest = rows - first
    second = rest.astype(jnp.bfloat16).astype(jnp.float32)
    third = rest - second
    parts = jnp.concatenate([first, second, third, jnp.zeros_like(first)], axis=0)
    places = lax.broadcasted_iota(jnp.int32, (rows.shape[1], indices.shape[1]), 0)
    chosen = jnp.where(places == indices, 1.0, 0.0).astype(jnp.bfloat16)
    picked = jnp.dot(parts.astype(jnp.bfloat16), chosen, preferred_element_type=jnp.float32)
    count = rows.shape[0]
    return picked[:count] + picked[count : 2 * count] + picked[2 * count : 3 * count]


def kernel(
    n_seg,
    n_band,
    scale,
    sft_hbm,
    doppler_hbm,
    antenna_hbm,
    index_hbm,
    offset_hbm,
    wing_hbm,
    out_ref,
    sft_ref,
    doppler_ref,
    antenna_ref,
    index_ref,
    offset_ref,
    wing_ref,
    x_ref,
    edge_ref,
    param_ref,
    fine_ref,
    column_ref,
    kernel_ref,
    part_ref,
    recv_ref,
    load_sem,
    edge_send,
    edge_recv,
    part_send,
    part_recv,
):
    seg = lax.axis_index("seg")
    band = lax.axis_index("band")
    segs_here, dets, _, bins = sft_ref.shape
    fine = index_ref.shape[1]
    own = fine // n_seg
    lines = 2 * dets
    has_up = band < n_band - 1
    has_down = band > 0
    up = jnp.minimum(band + 1, n_band - 1)
    down = jnp.maximum(band - 1, 0)

    barrier = pltpu.get_barrier_semaphore()
    for there, neighbour in ((has_up, up), (has_down, down)):

        @pl.when(there)
        def _():
            pl.semaphore_signal(
                barrier, inc=1, device_id={"band": neighbour}, device_id_type=MESH
            )

    for step in range(1, n_seg):
        pl.semaphore_signal(
            barrier,
            inc=1,
            device_id={"seg": lax.rem(seg + step, n_seg)},
            device_id_type=MESH,
        )

    loads = []
    for source, target in (
        (sft_hbm, sft_ref),
        (doppler_hbm, doppler_ref),
        (antenna_hbm, antenna_ref),
        (index_hbm, index_ref),
        (offset_hbm, offset_ref),
        (wing_hbm, wing_ref),
    ):
        loads.append(pltpu.make_async_copy(source, target, load_sem.at[len(loads)]))
        loads[-1].start()
    loads[0].wait()
    for s in range(segs_here):
        for d in range(dets):
            first = s * lines + 2 * d
            x_ref[first : first + 2, :] = sft_ref[s, d].astype(jnp.float32)
    neighbours = n_seg - 1 + has_up.astype(jnp.int32) + has_down.astype(jnp.int32)
    pl.semaphore_wait(barrier, neighbours)

    def edge_copy(side):
        start, neighbour = ((bins - LANES, up), (0, down))[side]
        return pltpu.make_async_remote_copy(
            src_ref=x_ref.at[:, pl.ds(start, LANES)],
            dst_ref=edge_ref.at[side],
            send_sem=edge_send.at[side],
            recv_sem=edge_recv.at[side],
            device_id={"band": neighbour},
            device_id_type=MESH,
        )

    for side, there in enumerate((has_up, has_down)):

        @pl.when(there)
        def _():
            edge_copy(side).start()

    for load in loads[1:]:
        load.wait()
    param_ref[...] = jnp.zeros_like(param_ref)
    fine_ref[...] = jnp.zeros_like(fine_ref)
    for s in range(segs_here):
        param_ref[ROWS * s : ROWS * s + 1, :] = doppler_ref[s : s + 1, :]
        for q in range(2):
            first = ROWS * s + 1 + dets * q
            param_ref[first : first + dets, :] = antenna_ref[s, q]
    for s in range(segs_here):
        rows = gathered_rows(param_ref[ROWS * s : ROWS * (s + 1), :], index_ref[s : s + 1, :])
        fine_ref[ROWS * s : ROWS * (s + 1), :] = rows
        sine, cosine = half_turn(rows[0:1])
        fine_ref[ROWS * s + 5 : ROWS * s + 6, :] = offset_ref[s : s + 1, :].astype(jnp.float32)
        fine_ref[ROWS * s + 6 : ROWS * s + 7, :] = sine
        fine_ref[ROWS * s + 7 : ROWS * s + 8, :] = cosine
    columns = jnp.transpose(fine_ref[...])
    column_ref[...] = columns

    lane = lax.broadcasted_iota(jnp.int32, (fine, 2 * TAPS), 1)
    from_real = lane < TAPS
    tap = (WMAX - 1 - lax.rem(lane, TAPS)).astype(jnp.float32)
    for s in range(segs_here):
        column = lambda row: columns[:, ROWS * s + row : ROWS * s + row + 1]
        u = tap - column(0)
        centre = u == 0.0
        envelope = jnp.where(
            centre, 1.0, -column(6) / jnp.where(centre, 1.0, math.pi * u)
        )
        real_part = envelope * column(7)
        imag_part = envelope * column(6)
        to_real = jnp.where(from_real, real_part, -imag_part)
        to_imag = jnp.where(from_real, imag_part, real_part)
        for q in range(2):
            for part, shape in enumerate((to_real, to_imag)):
                for d in range(dets):
                    piece = column(1 + dets * q + d) * shape
                    kernel_ref[s, 2 * q + part, :, 2 * TAPS * d : 2 * TAPS * (d + 1)] = (
                        piece.astype(jnp.bfloat16)
                    )

    width = bins + 2 * (WMAX + OMAX)
    wing_low = jnp.where(has_down, wing_ref[down], 0)
    wing_mid = wing_ref[band]
    wing_high = jnp.where(has_up, wing_ref[up], 0)
    position = lax.broadcasted_iota(jnp.int32, (TAPS, width), 1)
    reach = jnp.where(
        position < OMAX, wing_low, jnp.where(position < OMAX + bins, wing_mid, wing_high)
    )
    tap_here = WMAX - 1 - lax.broadcasted_iota(jnp.int32, (TAPS, width), 0)
    inside = (tap_here >= -reach) & (tap_here < reach)

    for side, there in enumerate((has_down, has_up)):

        @pl.when(there)
        def _():
            edge_copy(side).wait_recv()

    low = jnp.where(has_down, edge_ref[0], 0.0)
    high = jnp.where(has_up, edge_ref[1], 0.0)
    padded = jnp.concatenate([low, x_ref[...], high], axis=1)
    margin = LANES - WMAX - OMAX
    padded = pltpu.roll(padded, padded.shape[1] - margin, 1)[:, :width]

    transforms = []
    for s in range(segs_here):
        unfolded = []
        for line in range(s * lines, (s + 1) * lines):
            spread = jnp.broadcast_to(padded[line : line + 1, :], (TAPS, width))
            spread = pltpu.roll(spread, width - TAPS + 1, 1, stride=1, stride_axis=0)
            unfolded.append(jnp.where(inside, spread, 0.0))
        transforms.append(jnp.concatenate(unfolded, axis=0).astype(jnp.bfloat16))

    def fine_block(owner):
        rows = pl.ds(pl.multiple_of(owner * own, own), own)
        columns = column_ref[rows, :]
        total = None
        for s in range(segs_here):
            taps = jnp.concatenate([kernel_ref[s, part, rows, :] for part in range(4)], axis=0)
            amplitude = jnp.dot(taps, transforms[s], preferred_element_type=jnp.float32)
            power = amplitude * amplitude
            coarse = (power[:own] + power[own : 2 * own]) + (
                power[2 * own : 3 * own] + power[3 * own :]
            )
            shift = columns[:, ROWS * s + 5 : ROWS * s + 6].astype(jnp.int32) + OMAX
            for bit in range((2 * OMAX).bit_length()):
                moved = pltpu.roll(coarse, width - (1 << bit), 1)
                coarse = jnp.where((shift & (1 << bit)) != 0, moved, coarse)
            total = coarse[:, :bins] if total is None else total + coarse[:, :bins]
        return total * scale

    sends = []
    for step in range(1, n_seg):
        peer = lax.rem(seg + step, n_seg)
        part_ref[step - 1] = fine_block(peer)
        sends.append(
            pltpu.make_async_remote_copy(
                src_ref=part_ref.at[step - 1],
                dst_ref=recv_ref.at[step - 1],
                send_sem=part_send.at[step - 1],
                recv_sem=part_recv.at[step - 1],
                device_id={"seg": peer},
                device_id_type=MESH,
            )
        )
        sends[-1].start()
    result = fine_block(seg)
    for step in range(1, n_seg):
        sends[step - 1].wait_recv()
        result = result + recv_ref[step - 1]
    out_ref[...] = result
    for send in sends:
        send.wait_send()
    for side, there in enumerate((has_up, has_down)):

        @pl.when(there)
        def _():
            edge_copy(side).wait_send()


def solution(mesh):
    n_seg = mesh.shape["seg"]
    n_band = mesh.shape["band"]
    placed = (
        P("seg", None, None, "band"),
        P("seg", None),
        P("seg", None, None, None),
        P("seg", None),
        P("seg", None),
        P(),
    )

    def per_device(sft, doppler, antenna, coarse_index, freq_offset, wing_width):
        segs_here, dets, _, bins = sft.shape
        fine = coarse_index.shape[1]
        own = fine // n_seg
        lines = segs_here * dets * 2
        operands = [
            pltpu.with_memory_space_constraint(operand, pltpu.HBM)
            for operand in (sft, doppler, antenna, coarse_index, freq_offset, wing_width)
        ]
        vmem = pl.BlockSpec(memory_space=pltpu.VMEM)
        hbm = pl.BlockSpec(memory_space=pltpu.HBM)
        return pl.pallas_call(
            functools.partial(kernel, n_seg, n_band, 0.25 / (segs_here * n_seg)),
            out_shape=jax.ShapeDtypeStruct((own, bins), jnp.float32),
            in_specs=[hbm] * 6,
            out_specs=vmem,
            scratch_shapes=[
                pltpu.VMEM(sft.shape, sft.dtype),
                pltpu.VMEM(doppler.shape, doppler.dtype),
                pltpu.VMEM(antenna.shape, antenna.dtype),
                pltpu.VMEM(coarse_index.shape, coarse_index.dtype),
                pltpu.VMEM(freq_offset.shape, freq_offset.dtype),
                pltpu.SMEM(wing_width.shape, wing_width.dtype),
                pltpu.VMEM((lines, bins), jnp.float32),
                pltpu.VMEM((2, lines, LANES), jnp.float32),
                pltpu.VMEM((ROWS * segs_here, doppler.shape[1]), jnp.float32),
                pltpu.VMEM((LANES, fine), jnp.float32),
                pltpu.VMEM((fine, LANES), jnp.float32),
                pltpu.VMEM((segs_here, 4, fine, 2 * TAPS * dets), jnp.bfloat16),
                pltpu.VMEM((n_seg - 1, own, bins), jnp.float32),
                pltpu.VMEM((n_seg - 1, own, bins), jnp.float32),
                pltpu.SemaphoreType.DMA((6,)),
                pltpu.SemaphoreType.DMA((2,)),
                pltpu.SemaphoreType.DMA((2,)),
                pltpu.SemaphoreType.DMA((n_seg - 1,)),
                pltpu.SemaphoreType.DMA((n_seg - 1,)),
            ],
            compiler_params=pltpu.CompilerParams(
                collective_id=0, has_side_effects=True, vmem_limit_bytes=40 * 1024 * 1024
            ),
        )(*operands)

    return jax.shard_map(
        per_device, mesh=mesh, in_specs=placed, out_specs=P("seg", "band"), check_vma=False
    )
```

```python
import functools
import math

import jax
import jax.numpy as jnp
from jax import lax
from jax.experimental import pallas as pl
from jax.experimental.pallas import tpu as pltpu
from jax.sharding import PartitionSpec as P

WMAX = 32
OMAX = 32
TAPS = 2 * WMAX
LANES = 128
ROWS = 8
MESH = pl.DeviceIdType.MESH


def half_turn(x):
    rest = x - jnp.round(x)
    angle = rest * math.pi
    square = angle * angle
    sine = jnp.zeros_like(x)
    cosine = jnp.zeros_like(x)
    for power in range(7, -1, -1):
        sign = -1.0 if power % 2 else 1.0
        cosine = cosine * square + sign / math.factorial(2 * power)
        sine = sine * square + sign / math.factorial(2 * power + 1)
    return sine * angle, cosine


def gathered_rows(rows, indices):
    first = rows.astype(jnp.bfloat16).astype(jnp.float32)
    rest = rows - first
    second = rest.astype(jnp.bfloat16).astype(jnp.float32)
    third = rest - second
    parts = jnp.concatenate([first, second, third, jnp.zeros_like(first)], axis=0)
    places = lax.broadcasted_iota(jnp.int32, (rows.shape[1], indices.shape[1]), 0)
    chosen = jnp.where(places == indices, 1.0, 0.0).astype(jnp.bfloat16)
    picked = jnp.dot(parts.astype(jnp.bfloat16), chosen, preferred_element_type=jnp.float32)
    count = rows.shape[0]
    return picked[:count] + picked[count : 2 * count] + picked[2 * count : 3 * count]


def kernel(
    n_seg,
    n_band,
    scale,
    sft_hbm,
    doppler_hbm,
    antenna_hbm,
    index_hbm,
    offset_hbm,
    wing_hbm,
    out_ref,
    sft_ref,
    doppler_ref,
    antenna_ref,
    index_ref,
    offset_ref,
    wing_ref,
    param_ref,
    fine_ref,
    column_ref,
    x_ref,
    edge_ref,
    block_ref,
    load_sem,
    x_send,
    x_recv,
    edge_send,
    edge_recv,
    block_send,
    block_recv,
):
    seg = lax.axis_index("seg")
    band = lax.axis_index("band")
    segs_here, dets, _, bins = sft_ref.shape
    fine = index_ref.shape[1]
    own = fine // n_seg
    lines = 2 * dets
    has_up = band < n_band - 1
    has_down = band > 0
    up = jnp.minimum(band + 1, n_band - 1)
    down = jnp.maximum(band - 1, 0)
    peers = [lax.rem(seg + step, n_seg) for step in range(n_seg)]

    barrier = pltpu.get_barrier_semaphore()

    def greet(peer, there):
        pl.semaphore_signal(
            barrier, inc=1, device_id={"seg": peer, "band": there}, device_id_type=MESH
        )

    for peer in peers[1:]:
        greet(peer, band)
    for there, neighbour in ((has_up, up), (has_down, down)):

        @pl.when(there)
        def _():
            for peer in peers:
                greet(peer, neighbour)

    loads = []
    for source, target in (
        (sft_hbm, sft_ref),
        (doppler_hbm, doppler_ref),
        (antenna_hbm, antenna_ref),
        (index_hbm, index_ref),
        (offset_hbm, offset_ref),
        (wing_hbm, wing_ref),
    ):
        loads.append(pltpu.make_async_copy(source, target, load_sem.at[len(loads)]))
        loads[-1].start()
    loads[0].wait()
    for s in range(segs_here):
        for d in range(dets):
            first = s * lines + 2 * d
            x_ref[0, first : first + 2, :] = sft_ref[s, d].astype(jnp.float32)
    sides = has_up.astype(jnp.int32) + has_down.astype(jnp.int32)
    pl.semaphore_wait(barrier, n_seg - 1 + n_seg * sides)

    def edge_copy(side, step):
        start, neighbour = ((bins - LANES, up), (0, down))[side]
        return pltpu.make_async_remote_copy(
            src_ref=x_ref.at[0, :, pl.ds(start, LANES)],
            dst_ref=edge_ref.at[step, side],
            send_sem=edge_send.at[side, step],
            recv_sem=edge_recv.at[side, step],
            device_id={"seg": peers[step], "band": neighbour},
            device_id_type=MESH,
        )

    def x_copy(step):
        return pltpu.make_async_remote_copy(
            src_ref=x_ref.at[0],
            dst_ref=x_ref.at[step],
            send_sem=x_send.at[step - 1],
            recv_sem=x_recv.at[step - 1],
            device_id={"seg": peers[step], "band": band},
            device_id_type=MESH,
        )

    def block_copy(step):
        return pltpu.make_async_remote_copy(
            src_ref=column_ref.at[pl.ds(pl.multiple_of(peers[step] * own, own), own)],
            dst_ref=block_ref.at[step - 1],
            send_sem=block_send.at[step - 1],
            recv_sem=block_recv.at[step - 1],
            device_id={"seg": peers[step], "band": band},
            device_id_type=MESH,
        )

    for side, there in enumerate((has_up, has_down)):

        @pl.when(there)
        def _():
            for step in range(n_seg):
                edge_copy(side, step).start()

    for step in range(1, n_seg):
        x_copy(step).start()

    for load in loads[1:]:
        load.wait()
    param_ref[...] = jnp.zeros_like(param_ref)
    fine_ref[...] = jnp.zeros_like(fine_ref)
    for s in range(segs_here):
        param_ref[ROWS * s : ROWS * s + 1, :] = doppler_ref[s : s + 1, :]
        for q in range(2):
            first = ROWS * s + 1 + dets * q
            param_ref[first : first + dets, :] = antenna_ref[s, q]
    for s in range(segs_here):
        rows = gathered_rows(param_ref[ROWS * s : ROWS * (s + 1), :], index_ref[s : s + 1, :])
        fine_ref[ROWS * s : ROWS * (s + 1), :] = rows
        sine, cosine = half_turn(rows[0:1])
        fine_ref[ROWS * s + 5 : ROWS * s + 6, :] = offset_ref[s : s + 1, :].astype(jnp.float32)
        fine_ref[ROWS * s + 6 : ROWS * s + 7, :] = sine
        fine_ref[ROWS * s + 7 : ROWS * s + 8, :] = cosine
    column_ref[...] = jnp.transpose(fine_ref[...])
    for step in range(1, n_seg):
        block_copy(step).start()

    width = bins + 2 * (WMAX + OMAX)
    wing_low = jnp.where(has_down, wing_ref[down], 0)
    wing_mid = wing_ref[band]
    wing_high = jnp.where(has_up, wing_ref[up], 0)
    position = lax.broadcasted_iota(jnp.int32, (TAPS, width), 1)
    reach = jnp.where(
        position < OMAX, wing_low, jnp.where(position < OMAX + bins, wing_mid, wing_high)
    )
    tap_here = WMAX - 1 - lax.broadcasted_iota(jnp.int32, (TAPS, width), 0)
    inside = jnp.where((tap_here >= -reach) & (tap_here < reach), 1.0, 0.0).astype(jnp.bfloat16)

    lane = lax.broadcasted_iota(jnp.int32, (own, 2 * TAPS), 1)
    from_real = lane < TAPS
    tap = (WMAX - 1 - lax.rem(lane, TAPS)).astype(jnp.float32)

    def demodulators(columns, s):
        column = lambda row: columns[:, ROWS * s + row : ROWS * s + row + 1]
        u = tap - column(0)
        centre = u == 0.0
        envelope = jnp.where(
            centre, 1.0, -column(6) / jnp.where(centre, 1.0, math.pi * u)
        )
        real_part = envelope * column(7)
        imag_part = envelope * column(6)
        to_real = jnp.where(from_real, real_part, -imag_part)
        to_imag = jnp.where(from_real, imag_part, real_part)
        blocks = []
        for q in range(2):
            for shape in (to_real, to_imag):
                pieces = [column(1 + dets * q + d) * shape for d in range(dets)]
                blocks.append(jnp.concatenate(pieces, axis=1))
        return jnp.concatenate(blocks, axis=0).astype(jnp.bfloat16)

    total = jnp.zeros((own, bins), jnp.float32)
    for step in range(n_seg):
        if step == 0:
            columns = column_ref[pl.ds(pl.multiple_of(seg * own, own), own), :]
        else:
            block_copy(step).wait_recv()
            columns = block_ref[step - 1]
        kernels = [demodulators(columns, s) for s in range(segs_here)]
        for side, there in enumerate((has_down, has_up)):

            @pl.when(there)
            def _():
                edge_copy(side, step).wait_recv()

        if step > 0:
            x_copy(step).wait_recv()
        low = jnp.where(has_down, edge_ref[step, 0], 0.0)
        high = jnp.where(has_up, edge_ref[step, 1], 0.0)
        padded = jnp.concatenate([low, x_ref[step], high], axis=1)
        margin = LANES - WMAX - OMAX
        padded = pltpu.roll(padded, padded.shape[1] - margin, 1)[:, :width]
        for s in range(segs_here):
            unfolded = []
            for line in range(s * lines, (s + 1) * lines):
                spread = jnp.broadcast_to(padded[line : line + 1, :], (TAPS, width))
                spread = pltpu.roll(spread, width - TAPS + 1, 1, stride=1, stride_axis=0)
                unfolded.append(spread.astype(jnp.bfloat16) * inside)
            unfolded = jnp.concatenate(unfolded, axis=0)
            amplitude = jnp.dot(kernels[s], unfolded, preferred_element_type=jnp.float32)
            power = amplitude * amplitude
            coarse = (power[:own] + power[own : 2 * own]) + (
                power[2 * own : 3 * own] + power[3 * own :]
            )
            shift = columns[:, ROWS * s + 5 : ROWS * s + 6].astype(jnp.int32) + OMAX
            for bit in range((2 * OMAX).bit_length()):
                moved = pltpu.roll(coarse, width - (1 << bit), 1)
                coarse = jnp.where((shift & (1 << bit)) != 0, moved, coarse)
            total = total + coarse[:, :bins]
    out_ref[...] = total * scale

    for step in range(1, n_seg):
        x_copy(step).wait_send()
        block_copy(step).wait_send()
    for side, there in enumerate((has_up, has_down)):

        @pl.when(there)
        def _():
            for step in range(n_seg):
                edge_copy(side, step).wait_send()


def solution(mesh):
    n_seg = mesh.shape["seg"]
    n_band = mesh.shape["band"]
    placed = (
        P("seg", None, None, "band"),
        P("seg", None),
        P("seg", None, None, None),
        P("seg", None),
        P("seg", None),
        P(),
    )

    def per_device(sft, doppler, antenna, coarse_index, freq_offset, wing_width):
        segs_here, dets, _, bins = sft.shape
        fine = coarse_index.shape[1]
        own = fine // n_seg
        lines = segs_here * dets * 2
        operands = [
            pltpu.with_memory_space_constraint(operand, pltpu.HBM)
            for operand in (sft, doppler, antenna, coarse_index, freq_offset, wing_width)
        ]
        vmem = pl.BlockSpec(memory_space=pltpu.VMEM)
        hbm = pl.BlockSpec(memory_space=pltpu.HBM)
        return pl.pallas_call(
            functools.partial(kernel, n_seg, n_band, 0.25 / (segs_here * n_seg)),
            out_shape=jax.ShapeDtypeStruct((own, bins), jnp.float32),
            in_specs=[hbm] * 6,
            out_specs=vmem,
            scratch_shapes=[
                pltpu.VMEM(sft.shape, sft.dtype),
                pltpu.VMEM(doppler.shape, doppler.dtype),
                pltpu.VMEM(antenna.shape, antenna.dtype),
                pltpu.VMEM(coarse_index.shape, coarse_index.dtype),
                pltpu.VMEM(freq_offset.shape, freq_offset.dtype),
                pltpu.SMEM(wing_width.shape, wing_width.dtype),
                pltpu.VMEM((ROWS * segs_here, doppler.shape[1]), jnp.float32),
                pltpu.VMEM((LANES, fine), jnp.float32),
                pltpu.VMEM((fine, LANES), jnp.float32),
                pltpu.VMEM((n_seg, lines, bins), jnp.float32),
                pltpu.VMEM((n_seg, 2, lines, LANES), jnp.float32),
                pltpu.VMEM((n_seg - 1, own, LANES), jnp.float32),
                pltpu.SemaphoreType.DMA((6,)),
                pltpu.SemaphoreType.DMA((n_seg - 1,)),
                pltpu.SemaphoreType.DMA((n_seg - 1,)),
                pltpu.SemaphoreType.DMA((2, n_seg)),
                pltpu.SemaphoreType.DMA((2, n_seg)),
                pltpu.SemaphoreType.DMA((n_seg - 1,)),
                pltpu.SemaphoreType.DMA((n_seg - 1,)),
            ],
            compiler_params=pltpu.CompilerParams(
                collective_id=0, has_side_effects=True, vmem_limit_bytes=40 * 1024 * 1024
            ),
        )(*operands)

    return jax.shard_map(
        per_device, mesh=mesh, in_specs=placed, out_specs=P("seg", "band"), check_vma=False
    )
```

```python
import functools
import math

import jax
import jax.numpy as jnp
from jax import lax
from jax.experimental import pallas as pl
from jax.experimental.pallas import tpu as pltpu
from jax.sharding import PartitionSpec as P

WMAX = 32
OMAX = 32
LANES = 128
ROWS = 8
MESH = pl.DeviceIdType.MESH


def half_turn(x):
    rest = x - jnp.round(x)
    angle = rest * math.pi
    square = angle * angle
    sine = jnp.zeros_like(x)
    cosine = jnp.zeros_like(x)
    for power in range(7, -1, -1):
        sign = -1.0 if power % 2 else 1.0
        cosine = cosine * square + sign / math.factorial(2 * power)
        sine = sine * square + sign / math.factorial(2 * power + 1)
    return sine * angle, cosine


def gathered_rows(rows, indices):
    first = rows.astype(jnp.bfloat16).astype(jnp.float32)
    rest = rows - first
    second = rest.astype(jnp.bfloat16).astype(jnp.float32)
    third = rest - second
    parts = jnp.concatenate([first, second, third, jnp.zeros_like(first)], axis=0)
    places = lax.broadcasted_iota(jnp.int32, (rows.shape[1], indices.shape[1]), 0)
    chosen = jnp.where(places == indices, 1.0, 0.0).astype(jnp.bfloat16)
    picked = jnp.dot(parts.astype(jnp.bfloat16), chosen, preferred_element_type=jnp.float32)
    count = rows.shape[0]
    return picked[:count] + picked[count : 2 * count] + picked[2 * count : 3 * count]


def kernel(
    n_seg,
    n_band,
    scale,
    sft_hbm,
    doppler_hbm,
    antenna_hbm,
    index_hbm,
    offset_hbm,
    wing_hbm,
    out_ref,
    sft_ref,
    doppler_ref,
    antenna_ref,
    index_ref,
    offset_ref,
    wing_ref,
    param_ref,
    fine_ref,
    column_ref,
    x_ref,
    edge_ref,
    block_ref,
    load_sem,
    x_send,
    x_recv,
    edge_send,
    edge_recv,
    block_send,
    block_recv,
):
    seg = lax.axis_index("seg")
    band = lax.axis_index("band")
    segs_here, dets, _, bins = sft_ref.shape
    fine = index_ref.shape[1]
    own = fine // n_seg
    lines = 2 * dets
    has_up = band < n_band - 1
    has_down = band > 0
    up = jnp.minimum(band + 1, n_band - 1)
    down = jnp.maximum(band - 1, 0)
    peers = [lax.rem(seg + step, n_seg) for step in range(n_seg)]

    barrier = pltpu.get_barrier_semaphore()

    def greet(peer, there):
        pl.semaphore_signal(
            barrier, inc=1, device_id={"seg": peer, "band": there}, device_id_type=MESH
        )

    for peer in peers[1:]:
        greet(peer, band)
    for there, neighbour in ((has_up, up), (has_down, down)):

        @pl.when(there)
        def _():
            for peer in peers:
                greet(peer, neighbour)

    loads = []
    for source, target in (
        (sft_hbm, sft_ref),
        (doppler_hbm, doppler_ref),
        (antenna_hbm, antenna_ref),
        (index_hbm, index_ref),
        (offset_hbm, offset_ref),
        (wing_hbm, wing_ref),
    ):
        loads.append(pltpu.make_async_copy(source, target, load_sem.at[len(loads)]))
        loads[-1].start()
    loads[0].wait()
    for s in range(segs_here):
        for d in range(dets):
            first = s * lines + 2 * d
            x_ref[0, first : first + 2, :] = sft_ref[s, d].astype(jnp.float32)
    sides = has_up.astype(jnp.int32) + has_down.astype(jnp.int32)
    pl.semaphore_wait(barrier, n_seg - 1 + n_seg * sides)

    def edge_copy(side, step):
        start, neighbour = ((bins - LANES, up), (0, down))[side]
        return pltpu.make_async_remote_copy(
            src_ref=x_ref.at[0, :, pl.ds(start, LANES)],
            dst_ref=edge_ref.at[step, side],
            send_sem=edge_send.at[side, step],
            recv_sem=edge_recv.at[side, step],
            device_id={"seg": peers[step], "band": neighbour},
            device_id_type=MESH,
        )

    def x_copy(step):
        return pltpu.make_async_remote_copy(
            src_ref=x_ref.at[0],
            dst_ref=x_ref.at[step],
            send_sem=x_send.at[step - 1],
            recv_sem=x_recv.at[step - 1],
            device_id={"seg": peers[step], "band": band},
            device_id_type=MESH,
        )

    def block_copy(step):
        return pltpu.make_async_remote_copy(
            src_ref=column_ref.at[pl.ds(pl.multiple_of(peers[step] * own, own), own)],
            dst_ref=block_ref.at[step - 1],
            send_sem=block_send.at[step - 1],
            recv_sem=block_recv.at[step - 1],
            device_id={"seg": peers[step], "band": band},
            device_id_type=MESH,
        )

    for side, there in enumerate((has_up, has_down)):

        @pl.when(there)
        def _():
            for step in range(n_seg):
                edge_copy(side, step).start()

    for step in range(1, n_seg):
        x_copy(step).start()

    for load in loads[1:]:
        load.wait()
    param_ref[...] = jnp.zeros_like(param_ref)
    fine_ref[...] = jnp.zeros_like(fine_ref)
    for s in range(segs_here):
        param_ref[ROWS * s : ROWS * s + 1, :] = doppler_ref[s : s + 1, :]
        for q in range(2):
            first = ROWS * s + 1 + dets * q
            param_ref[first : first + dets, :] = antenna_ref[s, q]
    for s in range(segs_here):
        rows = gathered_rows(param_ref[ROWS * s : ROWS * (s + 1), :], index_ref[s : s + 1, :])
        fine_ref[ROWS * s : ROWS * (s + 1), :] = rows
        sine, cosine = half_turn(rows[0:1])
        fine_ref[ROWS * s + 5 : ROWS * s + 6, :] = offset_ref[s : s + 1, :].astype(jnp.float32)
        fine_ref[ROWS * s + 6 : ROWS * s + 7, :] = sine
        fine_ref[ROWS * s + 7 : ROWS * s + 8, :] = cosine
    column_ref[...] = jnp.transpose(fine_ref[...])
    for step in range(1, n_seg):
        block_copy(step).start()

    span = 2 * (WMAX + OMAX)
    width = bins + span
    wing_low = jnp.where(has_down, wing_ref[down], 0).astype(jnp.float32)
    wing_mid = wing_ref[band].astype(jnp.float32)
    wing_high = jnp.where(has_up, wing_ref[up], 0).astype(jnp.float32)
    lane = lax.broadcasted_iota(jnp.int32, (own, span), 1)
    reach = (span // 2 - 1 - lane).astype(jnp.float32)
    place = lax.broadcasted_iota(jnp.int32, (own, bins), 1).astype(jnp.float32)

    def demodulators(columns, s):
        column = lambda row: columns[:, ROWS * s + row : ROWS * s + row + 1]
        offset = column(5)
        tap = reach - offset
        u = tap - column(0)
        centre = u == 0.0
        envelope = jnp.where(
            centre, 1.0, -column(6) / jnp.where(centre, 1.0, math.pi * u)
        )
        real_part = envelope * column(7)
        imag_part = envelope * column(6)
        blocks = []
        for wing in (wing_mid, jnp.where(offset < 0.0, wing_low, wing_high)):
            inside = (tap >= -wing) & (tap < wing)
            real = jnp.where(inside, real_part, 0.0)
            imag = jnp.where(inside, imag_part, 0.0)
            for q in range(2):
                to_real, to_imag = [], []
                for d in range(dets):
                    weight = column(1 + dets * q + d)
                    weighted_real = (weight * real).astype(jnp.bfloat16)
                    weighted_imag = (weight * imag).astype(jnp.bfloat16)
                    to_real += [weighted_real, -weighted_imag]
                    to_imag += [weighted_imag, weighted_real]
                blocks.append(jnp.concatenate(to_real, axis=1))
                blocks.append(jnp.concatenate(to_imag, axis=1))
        return jnp.concatenate(blocks, axis=0)

    def unfold(low, middle, high):
        padded = jnp.concatenate(
            [jnp.where(has_down, low, 0.0), middle, jnp.where(has_up, high, 0.0)], axis=1
        )
        margin = LANES - WMAX - OMAX
        padded = pltpu.roll(padded, padded.shape[1] - margin, 1)[:, :width]
        spreads = []
        for line in range(segs_here * lines):
            spread = jnp.broadcast_to(padded[line : line + 1, :], (span, width))
            spread = pltpu.roll(spread, width - span + 1, 1, stride=1, stride_axis=0)
            spreads.append(spread[:, :bins].astype(jnp.bfloat16))
        return [
            jnp.concatenate(spreads[s * lines : (s + 1) * lines], axis=0)
            for s in range(segs_here)
        ]

    def moved_coarse(columns, s, kernels, unfolded):
        amplitude = jnp.dot(kernels, unfolded, preferred_element_type=jnp.float32)
        power = amplitude * amplitude
        parts = [power[own * part : own * (part + 1)] for part in range(8)]
        middle = (parts[0] + parts[1]) + (parts[2] + parts[3])
        beside = (parts[4] + parts[5]) + (parts[6] + parts[7])
        there = place + columns[:, ROWS * s + 5 : ROWS * s + 6]
        return jnp.where((there >= 0.0) & (there < float(bins)), middle, beside)

    def segment_sum(columns, x_slot):
        unfolded = unfold(edge_ref[x_slot, 0], x_ref[x_slot], edge_ref[x_slot, 1])
        result = None
        for s in range(segs_here):
            term = moved_coarse(columns, s, demodulators(columns, s), unfolded[s])
            result = term if result is None else result + term
        return result

    def wait_edges(step):
        for side, there in enumerate((has_down, has_up)):

            @pl.when(there)
            def _():
                edge_copy(side, step).wait_recv()

    wait_edges(0)
    columns = column_ref[pl.ds(pl.multiple_of(seg * own, own), own), :]
    total = segment_sum(columns, 0)
    for step in range(1, n_seg):
        wait_edges(step)
        x_copy(step).wait_recv()
        block_copy(step).wait_recv()
    for step in range(1, n_seg):
        total = total + segment_sum(block_ref[step - 1], step)
    out_ref[...] = total * scale

    for step in range(1, n_seg):
        x_copy(step).wait_send()
        block_copy(step).wait_send()
    for side, there in enumerate((has_up, has_down)):

        @pl.when(there)
        def _():
            for step in range(n_seg):
                edge_copy(side, step).wait_send()


def solution(mesh):
    n_seg = mesh.shape["seg"]
    n_band = mesh.shape["band"]
    placed = (
        P("seg", None, None, "band"),
        P("seg", None),
        P("seg", None, None, None),
        P("seg", None),
        P("seg", None),
        P(),
    )

    def per_device(sft, doppler, antenna, coarse_index, freq_offset, wing_width):
        segs_here, dets, _, bins = sft.shape
        fine = coarse_index.shape[1]
        own = fine // n_seg
        lines = segs_here * dets * 2
        operands = [
            pltpu.with_memory_space_constraint(operand, pltpu.HBM)
            for operand in (sft, doppler, antenna, coarse_index, freq_offset, wing_width)
        ]
        vmem = pl.BlockSpec(memory_space=pltpu.VMEM)
        hbm = pl.BlockSpec(memory_space=pltpu.HBM)
        return pl.pallas_call(
            functools.partial(kernel, n_seg, n_band, 0.25 / (segs_here * n_seg)),
            out_shape=jax.ShapeDtypeStruct((own, bins), jnp.float32),
            in_specs=[hbm] * 6,
            out_specs=vmem,
            scratch_shapes=[
                pltpu.VMEM(sft.shape, sft.dtype),
                pltpu.VMEM(doppler.shape, doppler.dtype),
                pltpu.VMEM(antenna.shape, antenna.dtype),
                pltpu.VMEM(coarse_index.shape, coarse_index.dtype),
                pltpu.VMEM(freq_offset.shape, freq_offset.dtype),
                pltpu.SMEM(wing_width.shape, wing_width.dtype),
                pltpu.VMEM((ROWS * segs_here, doppler.shape[1]), jnp.float32),
                pltpu.VMEM((LANES, fine), jnp.float32),
                pltpu.VMEM((fine, LANES), jnp.float32),
                pltpu.VMEM((n_seg, lines, bins), jnp.float32),
                pltpu.VMEM((n_seg, 2, lines, LANES), jnp.float32),
                pltpu.VMEM((n_seg - 1, own, LANES), jnp.float32),
                pltpu.SemaphoreType.DMA((6,)),
                pltpu.SemaphoreType.DMA((n_seg - 1,)),
                pltpu.SemaphoreType.DMA((n_seg - 1,)),
                pltpu.SemaphoreType.DMA((2, n_seg)),
                pltpu.SemaphoreType.DMA((2, n_seg)),
                pltpu.SemaphoreType.DMA((n_seg - 1,)),
                pltpu.SemaphoreType.DMA((n_seg - 1,)),
            ],
            compiler_params=pltpu.CompilerParams(
                collective_id=0, has_side_effects=True, vmem_limit_bytes=40 * 1024 * 1024
            ),
        )(*operands)

    return jax.shard_map(
        per_device, mesh=mesh, in_specs=placed, out_specs=P("seg", "band"), check_vma=False
    )
```

```python
import functools
import math

import jax
import jax.numpy as jnp
from jax import lax
from jax.experimental import pallas as pl
from jax.experimental.pallas import tpu as pltpu
from jax.sharding import PartitionSpec as P

WMAX = 32
OMAX = 32
LANES = 128
ROWS = 8
MESH = pl.DeviceIdType.MESH


def half_turn(x):
    rest = x - jnp.round(x)
    angle = rest * math.pi
    square = angle * angle
    sine = jnp.zeros_like(x)
    cosine = jnp.zeros_like(x)
    for power in range(7, -1, -1):
        sign = -1.0 if power % 2 else 1.0
        cosine = cosine * square + sign / math.factorial(2 * power)
        sine = sine * square + sign / math.factorial(2 * power + 1)
    return sine * angle, cosine


def gathered_rows(rows, indices):
    first = rows.astype(jnp.bfloat16).astype(jnp.float32)
    rest = rows - first
    second = rest.astype(jnp.bfloat16).astype(jnp.float32)
    third = rest - second
    parts = jnp.concatenate([first, second, third, jnp.zeros_like(first)], axis=0)
    places = lax.broadcasted_iota(jnp.int32, (rows.shape[1], indices.shape[1]), 0)
    chosen = jnp.where(places == indices, 1.0, 0.0).astype(jnp.bfloat16)
    picked = jnp.dot(parts.astype(jnp.bfloat16), chosen, preferred_element_type=jnp.float32)
    count = rows.shape[0]
    return picked[:count] + picked[count : 2 * count] + picked[2 * count : 3 * count]


def kernel(
    n_seg,
    n_band,
    scale,
    sft_hbm,
    doppler_hbm,
    antenna_hbm,
    index_hbm,
    offset_hbm,
    wing_hbm,
    out_ref,
    sft_ref,
    doppler_ref,
    antenna_ref,
    index_ref,
    offset_ref,
    wing_ref,
    param_ref,
    fine_ref,
    column_ref,
    x_ref,
    edge_ref,
    block_ref,
    load_sem,
    x_send,
    x_recv,
    edge_send,
    edge_recv,
    block_send,
    block_recv,
):
    seg = lax.axis_index("seg")
    band = lax.axis_index("band")
    segs_here, dets, _, bins = sft_ref.shape
    fine = index_ref.shape[1]
    own = fine // n_seg
    lines = 2 * dets
    has_up = band < n_band - 1
    has_down = band > 0
    up = jnp.minimum(band + 1, n_band - 1)
    down = jnp.maximum(band - 1, 0)
    peers = [lax.rem(seg + step, n_seg) for step in range(n_seg)]

    barrier = pltpu.get_barrier_semaphore()

    def greet(peer, there):
        pl.semaphore_signal(
            barrier, inc=1, device_id={"seg": peer, "band": there}, device_id_type=MESH
        )

    for peer in peers[1:]:
        greet(peer, band)
    for there, neighbour in ((has_up, up), (has_down, down)):

        @pl.when(there)
        def _():
            for peer in peers:
                greet(peer, neighbour)

    loads = []
    for source, target in (
        (sft_hbm, sft_ref),
        (doppler_hbm, doppler_ref),
        (antenna_hbm, antenna_ref),
        (index_hbm, index_ref),
        (offset_hbm, offset_ref),
        (wing_hbm, wing_ref),
    ):
        loads.append(pltpu.make_async_copy(source, target, load_sem.at[len(loads)]))
        loads[-1].start()
    loads[0].wait()
    for s in range(segs_here):
        for d in range(dets):
            first = s * lines + 2 * d
            x_ref[0, first : first + 2, :] = sft_ref[s, d].astype(jnp.float32)
    for load in loads[1:]:
        load.wait()
    param_ref[...] = jnp.zeros_like(param_ref)
    fine_ref[...] = jnp.zeros_like(fine_ref)
    for s in range(segs_here):
        param_ref[ROWS * s : ROWS * s + 1, :] = doppler_ref[s : s + 1, :]
        for q in range(2):
            first = ROWS * s + 1 + dets * q
            param_ref[first : first + dets, :] = antenna_ref[s, q]
    for s in range(segs_here):
        rows = gathered_rows(param_ref[ROWS * s : ROWS * (s + 1), :], index_ref[s : s + 1, :])
        fine_ref[ROWS * s : ROWS * (s + 1), :] = rows
        sine, cosine = half_turn(rows[0:1])
        fine_ref[ROWS * s + 5 : ROWS * s + 6, :] = offset_ref[s : s + 1, :].astype(jnp.float32)
        fine_ref[ROWS * s + 6 : ROWS * s + 7, :] = sine
        fine_ref[ROWS * s + 7 : ROWS * s + 8, :] = cosine
    column_ref[...] = jnp.transpose(fine_ref[...])
    sides = has_up.astype(jnp.int32) + has_down.astype(jnp.int32)
    pl.semaphore_wait(barrier, n_seg - 1 + n_seg * sides)

    def edge_copy(side, step):
        start, neighbour = ((bins - LANES, up), (0, down))[side]
        return pltpu.make_async_remote_copy(
            src_ref=x_ref.at[0, :, pl.ds(start, LANES)],
            dst_ref=edge_ref.at[step, side],
            send_sem=edge_send.at[side, step],
            recv_sem=edge_recv.at[side, step],
            device_id={"seg": peers[step], "band": neighbour},
            device_id_type=MESH,
        )

    def x_copy(step):
        return pltpu.make_async_remote_copy(
            src_ref=x_ref.at[0],
            dst_ref=x_ref.at[step],
            send_sem=x_send.at[step - 1],
            recv_sem=x_recv.at[step - 1],
            device_id={"seg": peers[step], "band": band},
            device_id_type=MESH,
        )

    def block_copy(step):
        return pltpu.make_async_remote_copy(
            src_ref=column_ref.at[pl.ds(pl.multiple_of(peers[step] * own, own), own)],
            dst_ref=block_ref.at[step - 1],
            send_sem=block_send.at[step - 1],
            recv_sem=block_recv.at[step - 1],
            device_id={"seg": peers[step], "band": band},
            device_id_type=MESH,
        )

    for side, there in enumerate((has_up, has_down)):

        @pl.when(there)
        def _():
            for step in range(n_seg):
                edge_copy(side, step).start()

    for step in range(1, n_seg):
        x_copy(step).start()

    for step in range(1, n_seg):
        block_copy(step).start()

    span = 2 * (WMAX + OMAX)
    width = bins + span
    wing_low = jnp.where(has_down, wing_ref[down], 0).astype(jnp.float32)
    wing_mid = wing_ref[band].astype(jnp.float32)
    wing_high = jnp.where(has_up, wing_ref[up], 0).astype(jnp.float32)
    lane = lax.broadcasted_iota(jnp.int32, (own, span), 1)
    reach = (span // 2 - 1 - lane).astype(jnp.float32)
    place = lax.broadcasted_iota(jnp.int32, (own, bins), 1).astype(jnp.float32)

    def demodulators(columns, s):
        column = lambda row: columns[:, ROWS * s + row : ROWS * s + row + 1]
        offset = column(5)
        tap = reach - offset
        u = tap - column(0)
        centre = u == 0.0
        envelope = jnp.where(
            centre, 1.0, -column(6) / jnp.where(centre, 1.0, math.pi * u)
        )
        real_part = envelope * column(7)
        imag_part = envelope * column(6)
        blocks = []
        for wing in (wing_mid, jnp.where(offset < 0.0, wing_low, wing_high)):
            inside = (tap >= -wing) & (tap < wing)
            real = jnp.where(inside, real_part, 0.0)
            imag = jnp.where(inside, imag_part, 0.0)
            for q in range(2):
                to_real, to_imag = [], []
                for d in range(dets):
                    weight = column(1 + dets * q + d)
                    weighted_real = (weight * real).astype(jnp.bfloat16)
                    weighted_imag = (weight * imag).astype(jnp.bfloat16)
                    to_real += [weighted_real, -weighted_imag]
                    to_imag += [weighted_imag, weighted_real]
                blocks.append(jnp.concatenate(to_real, axis=1))
                blocks.append(jnp.concatenate(to_imag, axis=1))
        return jnp.concatenate(blocks, axis=0)

    def unfold(low, middle, high):
        padded = jnp.concatenate(
            [jnp.where(has_down, low, 0.0), middle, jnp.where(has_up, high, 0.0)], axis=1
        )
        margin = LANES - WMAX - OMAX
        padded = pltpu.roll(padded, padded.shape[1] - margin, 1)[:, :width]
        spreads = []
        for line in range(segs_here * lines):
            spread = jnp.broadcast_to(padded[line : line + 1, :], (span, width))
            spread = pltpu.roll(spread, width - span + 1, 1, stride=1, stride_axis=0)
            spreads.append(spread[:, :bins].astype(jnp.bfloat16))
        return [
            jnp.concatenate(spreads[s * lines : (s + 1) * lines], axis=0)
            for s in range(segs_here)
        ]

    def moved_coarse(columns, s, kernels, unfolded):
        amplitude = jnp.dot(kernels, unfolded, preferred_element_type=jnp.float32)
        power = amplitude * amplitude
        parts = [power[own * part : own * (part + 1)] for part in range(8)]
        middle = (parts[0] + parts[1]) + (parts[2] + parts[3])
        beside = (parts[4] + parts[5]) + (parts[6] + parts[7])
        there = place + columns[:, ROWS * s + 5 : ROWS * s + 6]
        return jnp.where((there >= 0.0) & (there < float(bins)), middle, beside)

    def segment_sum(columns, x_slot):
        unfolded = unfold(edge_ref[x_slot, 0], x_ref[x_slot], edge_ref[x_slot, 1])
        result = None
        for s in range(segs_here):
            term = moved_coarse(columns, s, demodulators(columns, s), unfolded[s])
            result = term if result is None else result + term
        return result

    def wait_edges(step):
        for side, there in enumerate((has_down, has_up)):

            @pl.when(there)
            def _():
                edge_copy(side, step).wait_recv()

    wait_edges(0)
    columns = column_ref[pl.ds(pl.multiple_of(seg * own, own), own), :]
    total = segment_sum(columns, 0)
    for step in range(1, n_seg):
        wait_edges(step)
        x_copy(step).wait_recv()
        block_copy(step).wait_recv()
    for step in range(1, n_seg):
        total = total + segment_sum(block_ref[step - 1], step)
    out_ref[...] = total * scale

    for step in range(1, n_seg):
        x_copy(step).wait_send()
        block_copy(step).wait_send()
    for side, there in enumerate((has_up, has_down)):

        @pl.when(there)
        def _():
            for step in range(n_seg):
                edge_copy(side, step).wait_send()


def solution(mesh):
    n_seg = mesh.shape["seg"]
    n_band = mesh.shape["band"]
    placed = (
        P("seg", None, None, "band"),
        P("seg", None),
        P("seg", None, None, None),
        P("seg", None),
        P("seg", None),
        P(),
    )

    def per_device(sft, doppler, antenna, coarse_index, freq_offset, wing_width):
        segs_here, dets, _, bins = sft.shape
        fine = coarse_index.shape[1]
        own = fine // n_seg
        lines = segs_here * dets * 2
        operands = [
            pltpu.with_memory_space_constraint(operand, pltpu.HBM)
            for operand in (sft, doppler, antenna, coarse_index, freq_offset, wing_width)
        ]
        vmem = pl.BlockSpec(memory_space=pltpu.VMEM)
        hbm = pl.BlockSpec(memory_space=pltpu.HBM)
        return pl.pallas_call(
            functools.partial(kernel, n_seg, n_band, 0.25 / (segs_here * n_seg)),
            out_shape=jax.ShapeDtypeStruct((own, bins), jnp.float32),
            in_specs=[hbm] * 6,
            out_specs=vmem,
            scratch_shapes=[
                pltpu.VMEM(sft.shape, sft.dtype),
                pltpu.VMEM(doppler.shape, doppler.dtype),
                pltpu.VMEM(antenna.shape, antenna.dtype),
                pltpu.VMEM(coarse_index.shape, coarse_index.dtype),
                pltpu.VMEM(freq_offset.shape, freq_offset.dtype),
                pltpu.SMEM(wing_width.shape, wing_width.dtype),
                pltpu.VMEM((ROWS * segs_here, doppler.shape[1]), jnp.float32),
                pltpu.VMEM((LANES, fine), jnp.float32),
                pltpu.VMEM((fine, LANES), jnp.float32),
                pltpu.VMEM((n_seg, lines, bins), jnp.float32),
                pltpu.VMEM((n_seg, 2, lines, LANES), jnp.float32),
                pltpu.VMEM((n_seg - 1, own, LANES), jnp.float32),
                pltpu.SemaphoreType.DMA((6,)),
                pltpu.SemaphoreType.DMA((n_seg - 1,)),
                pltpu.SemaphoreType.DMA((n_seg - 1,)),
                pltpu.SemaphoreType.DMA((2, n_seg)),
                pltpu.SemaphoreType.DMA((2, n_seg)),
                pltpu.SemaphoreType.DMA((n_seg - 1,)),
                pltpu.SemaphoreType.DMA((n_seg - 1,)),
            ],
            compiler_params=pltpu.CompilerParams(
                collective_id=0, has_side_effects=True, vmem_limit_bytes=40 * 1024 * 1024
            ),
        )(*operands)

    return jax.shard_map(
        per_device, mesh=mesh, in_specs=placed, out_specs=P("seg", "band"), check_vma=False
    )
```

```python
import functools
import math

import jax
import jax.numpy as jnp
from jax import lax
from jax.experimental import pallas as pl
from jax.experimental.pallas import tpu as pltpu
from jax.sharding import PartitionSpec as P

WMAX = 32
OMAX = 32
LANES = 128
ROWS = 8
MESH = pl.DeviceIdType.MESH


def half_turn(x):
    rest = x - jnp.round(x)
    angle = rest * math.pi
    square = angle * angle
    sine = jnp.zeros_like(x)
    cosine = jnp.zeros_like(x)
    for power in range(7, -1, -1):
        sign = -1.0 if power % 2 else 1.0
        cosine = cosine * square + sign / math.factorial(2 * power)
        sine = sine * square + sign / math.factorial(2 * power + 1)
    return sine * angle, cosine


def gathered_rows(rows, indices):
    first = rows.astype(jnp.bfloat16).astype(jnp.float32)
    rest = rows - first
    second = rest.astype(jnp.bfloat16).astype(jnp.float32)
    third = rest - second
    parts = jnp.concatenate([first, second, third, jnp.zeros_like(first)], axis=0)
    places = lax.broadcasted_iota(jnp.int32, (rows.shape[1], indices.shape[1]), 0)
    chosen = jnp.where(places == indices, 1.0, 0.0).astype(jnp.bfloat16)
    picked = jnp.dot(parts.astype(jnp.bfloat16), chosen, preferred_element_type=jnp.float32)
    count = rows.shape[0]
    return picked[:count] + picked[count : 2 * count] + picked[2 * count : 3 * count]


def kernel(
    n_seg,
    n_band,
    scale,
    sft_hbm,
    doppler_hbm,
    antenna_hbm,
    index_hbm,
    offset_hbm,
    wing_hbm,
    out_ref,
    sft_ref,
    doppler_ref,
    antenna_ref,
    index_ref,
    offset_ref,
    wing_ref,
    param_ref,
    fine_ref,
    column_ref,
    x_ref,
    edge_ref,
    block_ref,
    load_sem,
    x_send,
    x_recv,
    edge_send,
    edge_recv,
    block_send,
    block_recv,
):
    seg = lax.axis_index("seg")
    band = lax.axis_index("band")
    segs_here, dets, _, bins = sft_ref.shape
    fine = index_ref.shape[1]
    own = fine // n_seg
    lines = 2 * dets
    has_up = band < n_band - 1
    has_down = band > 0
    up = jnp.minimum(band + 1, n_band - 1)
    down = jnp.maximum(band - 1, 0)
    peers = [lax.rem(seg + step, n_seg) for step in range(n_seg)]

    barrier = pltpu.get_barrier_semaphore()

    def greet(peer, there):
        pl.semaphore_signal(
            barrier, inc=1, device_id={"seg": peer, "band": there}, device_id_type=MESH
        )

    for peer in peers[1:]:
        greet(peer, band)
    for there, neighbour in ((has_up, up), (has_down, down)):

        @pl.when(there)
        def _():
            for peer in peers:
                greet(peer, neighbour)

    loads = []
    for source, target in (
        (sft_hbm, sft_ref),
        (doppler_hbm, doppler_ref),
        (antenna_hbm, antenna_ref),
        (index_hbm, index_ref),
        (offset_hbm, offset_ref),
        (wing_hbm, wing_ref),
    ):
        loads.append(pltpu.make_async_copy(source, target, load_sem.at[len(loads)]))
        loads[-1].start()
    loads[0].wait()
    for s in range(segs_here):
        for d in range(dets):
            first = s * lines + 2 * d
            x_ref[0, first : first + 2, :] = sft_ref[s, d].astype(jnp.float32)
    for load in loads[1:]:
        load.wait()
    param_ref[...] = jnp.zeros_like(param_ref)
    fine_ref[...] = jnp.zeros_like(fine_ref)
    for s in range(segs_here):
        param_ref[ROWS * s : ROWS * s + 1, :] = doppler_ref[s : s + 1, :]
        for q in range(2):
            first = ROWS * s + 1 + dets * q
            param_ref[first : first + dets, :] = antenna_ref[s, q]
    for s in range(segs_here):
        rows = gathered_rows(param_ref[ROWS * s : ROWS * (s + 1), :], index_ref[s : s + 1, :])
        fine_ref[ROWS * s : ROWS * (s + 1), :] = rows
        sine, cosine = half_turn(rows[0:1])
        fine_ref[ROWS * s + 5 : ROWS * s + 6, :] = offset_ref[s : s + 1, :].astype(jnp.float32)
        fine_ref[ROWS * s + 6 : ROWS * s + 7, :] = sine
        fine_ref[ROWS * s + 7 : ROWS * s + 8, :] = cosine
    column_ref[...] = jnp.transpose(fine_ref[...])
    sides = has_up.astype(jnp.int32) + has_down.astype(jnp.int32)
    pl.semaphore_wait(barrier, n_seg - 1 + n_seg * sides)

    def edge_copy(side, step):
        start, neighbour = ((bins - LANES, up), (0, down))[side]
        return pltpu.make_async_remote_copy(
            src_ref=x_ref.at[0, :, pl.ds(start, LANES)],
            dst_ref=edge_ref.at[step, side],
            send_sem=edge_send.at[side, step],
            recv_sem=edge_recv.at[side, step],
            device_id={"seg": peers[step], "band": neighbour},
            device_id_type=MESH,
        )

    def x_copy(step):
        return pltpu.make_async_remote_copy(
            src_ref=x_ref.at[0],
            dst_ref=x_ref.at[step],
            send_sem=x_send.at[step - 1],
            recv_sem=x_recv.at[step - 1],
            device_id={"seg": peers[step], "band": band},
            device_id_type=MESH,
        )

    def block_copy(step):
        return pltpu.make_async_remote_copy(
            src_ref=column_ref.at[pl.ds(pl.multiple_of(peers[step] * own, own), own)],
            dst_ref=block_ref.at[step - 1],
            send_sem=block_send.at[step - 1],
            recv_sem=block_recv.at[step - 1],
            device_id={"seg": peers[step], "band": band},
            device_id_type=MESH,
        )

    for side, there in enumerate((has_up, has_down)):

        @pl.when(there)
        def _():
            for step in range(n_seg):
                edge_copy(side, step).start()

    for step in range(1, n_seg):
        x_copy(step).start()

    for step in range(1, n_seg):
        block_copy(step).start()

    span = 2 * (WMAX + OMAX)
    width = bins + span
    wing_low = jnp.where(has_down, wing_ref[down], 0).astype(jnp.float32)
    wing_mid = wing_ref[band].astype(jnp.float32)
    wing_high = jnp.where(has_up, wing_ref[up], 0).astype(jnp.float32)
    lane = lax.broadcasted_iota(jnp.int32, (own, span), 1)
    reach = (span // 2 - 1 - lane).astype(jnp.float32)
    place = lax.broadcasted_iota(jnp.int32, (own, bins), 1).astype(jnp.float32)

    def demodulators(columns, s):
        column = lambda row: columns[:, ROWS * s + row : ROWS * s + row + 1]
        offset = column(5)
        tap = reach - offset
        u = tap - column(0)
        centre = u == 0.0
        envelope = jnp.where(
            centre, 1.0, -column(6) / jnp.where(centre, 1.0, math.pi * u)
        )
        real_part = envelope * column(7)
        imag_part = envelope * column(6)
        blocks = []
        for wing in (wing_mid, jnp.where(offset < 0.0, wing_low, wing_high)):
            inside = (tap >= -wing) & (tap < wing)
            real = jnp.where(inside, real_part, 0.0)
            imag = jnp.where(inside, imag_part, 0.0)
            for q in range(2):
                to_real, to_imag = [], []
                for d in range(dets):
                    weight = column(1 + dets * q + d)
                    weighted_real = (weight * real).astype(jnp.bfloat16)
                    weighted_imag = (weight * imag).astype(jnp.bfloat16)
                    to_real += [weighted_real, -weighted_imag]
                    to_imag += [weighted_imag, weighted_real]
                blocks.append(jnp.concatenate(to_real, axis=1))
                blocks.append(jnp.concatenate(to_imag, axis=1))
        return jnp.concatenate(blocks, axis=0)

    def unfold(low, middle, high):
        padded = jnp.concatenate(
            [jnp.where(has_down, low, 0.0), middle, jnp.where(has_up, high, 0.0)], axis=1
        )
        margin = LANES - WMAX - OMAX
        group = 2 * ROWS
        padded = pltpu.roll(padded, padded.shape[1] - margin, 1)[:, :width]
        spreads = []
        for line in range(segs_here * lines):
            rows = jnp.broadcast_to(padded[line : line + 1, :], (group, width))
            rows = pltpu.roll(rows, 0, 1, stride=1, stride_axis=0).astype(jnp.bfloat16)
            pieces = [
                pltpu.roll(rows, width - span + 1 + first, 1)[:, :bins]
                for first in range(0, span, group)
            ]
            spreads.append(jnp.concatenate(pieces, axis=0))
        return [
            jnp.concatenate(spreads[s * lines : (s + 1) * lines], axis=0)
            for s in range(segs_here)
        ]

    def moved_coarse(columns, s, kernels, unfolded):
        amplitude = jnp.dot(kernels, unfolded, preferred_element_type=jnp.float32)
        power = amplitude * amplitude
        parts = [power[own * part : own * (part + 1)] for part in range(8)]
        middle = (parts[0] + parts[1]) + (parts[2] + parts[3])
        beside = (parts[4] + parts[5]) + (parts[6] + parts[7])
        there = place + columns[:, ROWS * s + 5 : ROWS * s + 6]
        return jnp.where((there >= 0.0) & (there < float(bins)), middle, beside)

    def segment_sum(columns, x_slot):
        unfolded = unfold(edge_ref[x_slot, 0], x_ref[x_slot], edge_ref[x_slot, 1])
        result = None
        for s in range(segs_here):
            term = moved_coarse(columns, s, demodulators(columns, s), unfolded[s])
            result = term if result is None else result + term
        return result

    def wait_edges(step):
        for side, there in enumerate((has_down, has_up)):

            @pl.when(there)
            def _():
                edge_copy(side, step).wait_recv()

    wait_edges(0)
    columns = column_ref[pl.ds(pl.multiple_of(seg * own, own), own), :]
    total = segment_sum(columns, 0)
    for step in range(1, n_seg):
        wait_edges(step)
        x_copy(step).wait_recv()
        block_copy(step).wait_recv()
    for step in range(1, n_seg):
        total = total + segment_sum(block_ref[step - 1], step)
    out_ref[...] = total * scale

    for step in range(1, n_seg):
        x_copy(step).wait_send()
        block_copy(step).wait_send()
    for side, there in enumerate((has_up, has_down)):

        @pl.when(there)
        def _():
            for step in range(n_seg):
                edge_copy(side, step).wait_send()


def solution(mesh):
    n_seg = mesh.shape["seg"]
    n_band = mesh.shape["band"]
    placed = (
        P("seg", None, None, "band"),
        P("seg", None),
        P("seg", None, None, None),
        P("seg", None),
        P("seg", None),
        P(),
    )

    def per_device(sft, doppler, antenna, coarse_index, freq_offset, wing_width):
        segs_here, dets, _, bins = sft.shape
        fine = coarse_index.shape[1]
        own = fine // n_seg
        lines = segs_here * dets * 2
        operands = [
            pltpu.with_memory_space_constraint(operand, pltpu.HBM)
            for operand in (sft, doppler, antenna, coarse_index, freq_offset, wing_width)
        ]
        vmem = pl.BlockSpec(memory_space=pltpu.VMEM)
        hbm = pl.BlockSpec(memory_space=pltpu.HBM)
        return pl.pallas_call(
            functools.partial(kernel, n_seg, n_band, 0.25 / (segs_here * n_seg)),
            out_shape=jax.ShapeDtypeStruct((own, bins), jnp.float32),
            in_specs=[hbm] * 6,
            out_specs=vmem,
            scratch_shapes=[
                pltpu.VMEM(sft.shape, sft.dtype),
                pltpu.VMEM(doppler.shape, doppler.dtype),
                pltpu.VMEM(antenna.shape, antenna.dtype),
                pltpu.VMEM(coarse_index.shape, coarse_index.dtype),
                pltpu.VMEM(freq_offset.shape, freq_offset.dtype),
                pltpu.SMEM(wing_width.shape, wing_width.dtype),
                pltpu.VMEM((ROWS * segs_here, doppler.shape[1]), jnp.float32),
                pltpu.VMEM((LANES, fine), jnp.float32),
                pltpu.VMEM((fine, LANES), jnp.float32),
                pltpu.VMEM((n_seg, lines, bins), jnp.float32),
                pltpu.VMEM((n_seg, 2, lines, LANES), jnp.float32),
                pltpu.VMEM((n_seg - 1, own, LANES), jnp.float32),
                pltpu.SemaphoreType.DMA((6,)),
                pltpu.SemaphoreType.DMA((n_seg - 1,)),
                pltpu.SemaphoreType.DMA((n_seg - 1,)),
                pltpu.SemaphoreType.DMA((2, n_seg)),
                pltpu.SemaphoreType.DMA((2, n_seg)),
                pltpu.SemaphoreType.DMA((n_seg - 1,)),
                pltpu.SemaphoreType.DMA((n_seg - 1,)),
            ],
            compiler_params=pltpu.CompilerParams(
                collective_id=0, has_side_effects=True, vmem_limit_bytes=40 * 1024 * 1024
            ),
        )(*operands)

    return jax.shard_map(
        per_device, mesh=mesh, in_specs=placed, out_specs=P("seg", "band"), check_vma=False
    )
```

```python
import functools
import math

import jax
import jax.numpy as jnp
from jax import lax
from jax.experimental import pallas as pl
from jax.experimental.pallas import tpu as pltpu
from jax.sharding import PartitionSpec as P

WMAX = 32
OMAX = 32
LANES = 128
ROWS = 8
MESH = pl.DeviceIdType.MESH


def half_turn(x):
    rest = x - jnp.round(x)
    angle = rest * math.pi
    square = angle * angle
    sine = jnp.zeros_like(x)
    cosine = jnp.zeros_like(x)
    for power in range(7, -1, -1):
        sign = -1.0 if power % 2 else 1.0
        cosine = cosine * square + sign / math.factorial(2 * power)
        sine = sine * square + sign / math.factorial(2 * power + 1)
    return sine * angle, cosine


def gathered_rows(rows, indices):
    first = rows.astype(jnp.bfloat16).astype(jnp.float32)
    rest = rows - first
    second = rest.astype(jnp.bfloat16).astype(jnp.float32)
    third = rest - second
    parts = jnp.concatenate([first, second, third, jnp.zeros_like(first)], axis=0)
    places = lax.broadcasted_iota(jnp.int32, (rows.shape[1], indices.shape[1]), 0)
    chosen = jnp.where(places == indices, 1.0, 0.0).astype(jnp.bfloat16)
    picked = jnp.dot(parts.astype(jnp.bfloat16), chosen, preferred_element_type=jnp.float32)
    count = rows.shape[0]
    return picked[:count] + picked[count : 2 * count] + picked[2 * count : 3 * count]


def kernel(
    n_seg,
    n_band,
    scale,
    sft_hbm,
    doppler_hbm,
    antenna_hbm,
    index_hbm,
    offset_hbm,
    wing_hbm,
    out_ref,
    sft_ref,
    doppler_ref,
    antenna_ref,
    index_ref,
    offset_ref,
    wing_ref,
    x_ref,
    edge_ref,
    param_ref,
    fine_ref,
    column_ref,
    kernel_ref,
    part_ref,
    recv_ref,
    load_sem,
    edge_send,
    edge_recv,
    part_send,
    part_recv,
):
    seg = lax.axis_index("seg")
    band = lax.axis_index("band")
    segs_here, dets, _, bins = sft_ref.shape
    fine = index_ref.shape[1]
    own = fine // n_seg
    lines = 2 * dets
    has_up = band < n_band - 1
    has_down = band > 0
    up = jnp.minimum(band + 1, n_band - 1)
    down = jnp.maximum(band - 1, 0)

    barrier = pltpu.get_barrier_semaphore()
    for there, neighbour in ((has_up, up), (has_down, down)):

        @pl.when(there)
        def _():
            pl.semaphore_signal(
                barrier, inc=1, device_id={"band": neighbour}, device_id_type=MESH
            )

    for step in range(1, n_seg):
        pl.semaphore_signal(
            barrier,
            inc=1,
            device_id={"seg": lax.rem(seg + step, n_seg)},
            device_id_type=MESH,
        )

    loads = []
    for source, target in (
        (sft_hbm, sft_ref),
        (doppler_hbm, doppler_ref),
        (antenna_hbm, antenna_ref),
        (index_hbm, index_ref),
        (offset_hbm, offset_ref),
        (wing_hbm, wing_ref),
    ):
        loads.append(pltpu.make_async_copy(source, target, load_sem.at[len(loads)]))
        loads[-1].start()
    loads[0].wait()
    for s in range(segs_here):
        for d in range(dets):
            first = s * lines + 2 * d
            x_ref[first : first + 2, :] = sft_ref[s, d].astype(jnp.float32)
    neighbours = n_seg - 1 + has_up.astype(jnp.int32) + has_down.astype(jnp.int32)
    pl.semaphore_wait(barrier, neighbours)

    def edge_copy(side):
        start, neighbour = ((bins - LANES, up), (0, down))[side]
        return pltpu.make_async_remote_copy(
            src_ref=x_ref.at[:, pl.ds(start, LANES)],
            dst_ref=edge_ref.at[side],
            send_sem=edge_send.at[side],
            recv_sem=edge_recv.at[side],
            device_id={"band": neighbour},
            device_id_type=MESH,
        )

    for side, there in enumerate((has_up, has_down)):

        @pl.when(there)
        def _():
            edge_copy(side).start()

    for load in loads[1:]:
        load.wait()
    param_ref[...] = jnp.zeros_like(param_ref)
    fine_ref[...] = jnp.zeros_like(fine_ref)
    for s in range(segs_here):
        param_ref[ROWS * s : ROWS * s + 1, :] = doppler_ref[s : s + 1, :]
        for q in range(2):
            first = ROWS * s + 1 + dets * q
            param_ref[first : first + dets, :] = antenna_ref[s, q]
    for s in range(segs_here):
        rows = gathered_rows(param_ref[ROWS * s : ROWS * (s + 1), :], index_ref[s : s + 1, :])
        fine_ref[ROWS * s : ROWS * (s + 1), :] = rows
        sine, cosine = half_turn(rows[0:1])
        fine_ref[ROWS * s + 5 : ROWS * s + 6, :] = offset_ref[s : s + 1, :].astype(jnp.float32)
        fine_ref[ROWS * s + 6 : ROWS * s + 7, :] = sine
        fine_ref[ROWS * s + 7 : ROWS * s + 8, :] = cosine
    columns = jnp.transpose(fine_ref[...])
    column_ref[...] = columns

    span = 2 * (WMAX + OMAX)
    width = bins + span
    wing_low = jnp.where(has_down, wing_ref[down], 0).astype(jnp.float32)
    wing_mid = wing_ref[band].astype(jnp.float32)
    wing_high = jnp.where(has_up, wing_ref[up], 0).astype(jnp.float32)
    lane = lax.broadcasted_iota(jnp.int32, (fine, span), 1)
    reach = (span // 2 - 1 - lane).astype(jnp.float32)
    place = lax.broadcasted_iota(jnp.int32, (own, bins), 1).astype(jnp.float32)

    def store_demodulators(columns, s):
        column = lambda row: columns[:, ROWS * s + row : ROWS * s + row + 1]
        offset = column(5)
        tap = reach - offset
        u = tap - column(0)
        centre = u == 0.0
        envelope = jnp.where(
            centre, 1.0, -column(6) / jnp.where(centre, 1.0, math.pi * u)
        )
        real_part = envelope * column(7)
        imag_part = envelope * column(6)
        blocks = []
        for wing in (wing_mid, jnp.where(offset < 0.0, wing_low, wing_high)):
            inside = (tap >= -wing) & (tap < wing)
            real = jnp.where(inside, real_part, 0.0)
            imag = jnp.where(inside, imag_part, 0.0)
            for q in range(2):
                to_real, to_imag = [], []
                for d in range(dets):
                    weight = column(1 + dets * q + d)
                    weighted_real = (weight * real).astype(jnp.bfloat16)
                    weighted_imag = (weight * imag).astype(jnp.bfloat16)
                    to_real += [weighted_real, -weighted_imag]
                    to_imag += [weighted_imag, weighted_real]
                blocks.append(jnp.concatenate(to_real, axis=1))
                blocks.append(jnp.concatenate(to_imag, axis=1))
        for part, block in enumerate(blocks):
            kernel_ref[s, part] = block

    def unfold(low, middle, high):
        padded = jnp.concatenate(
            [jnp.where(has_down, low, 0.0), middle, jnp.where(has_up, high, 0.0)], axis=1
        )
        margin = LANES - WMAX - OMAX
        padded = pltpu.roll(padded, padded.shape[1] - margin, 1)[:, :width]
        spreads = []
        for line in range(segs_here * lines):
            spread = jnp.broadcast_to(padded[line : line + 1, :], (span, width))
            spread = pltpu.roll(spread, width - span + 1, 1, stride=1, stride_axis=0)
            spreads.append(spread[:, :bins].astype(jnp.bfloat16))
        return [
            jnp.concatenate(spreads[s * lines : (s + 1) * lines], axis=0)
            for s in range(segs_here)
        ]

    for s in range(segs_here):
        store_demodulators(columns, s)

    for side, there in enumerate((has_down, has_up)):

        @pl.when(there)
        def _():
            edge_copy(side).wait_recv()

    transforms = unfold(edge_ref[0], x_ref[...], edge_ref[1])

    def fine_blocks(owners):
        spans = [pl.ds(pl.multiple_of(owner * own, own), own) for owner in owners]
        totals = [None] * len(owners)
        for s in range(segs_here):
            taps = [kernel_ref[s, part, rows, :] for rows in spans for part in range(8)]
            amplitude = jnp.dot(
                jnp.concatenate(taps, axis=0), transforms[s], preferred_element_type=jnp.float32
            )
            power = amplitude * amplitude
            for at, rows in enumerate(spans):
                first = 8 * at
                parts = [power[own * part : own * (part + 1)] for part in range(first, first + 8)]
                middle = (parts[0] + parts[1]) + (parts[2] + parts[3])
                beside = (parts[4] + parts[5]) + (parts[6] + parts[7])
                there = place + column_ref[rows, ROWS * s + 5 : ROWS * s + 6]
                moved = jnp.where((there >= 0.0) & (there < float(bins)), middle, beside)
                totals[at] = moved if totals[at] is None else totals[at] + moved
        return [total * scale for total in totals]

    def part_copy(step):
        return pltpu.make_async_remote_copy(
            src_ref=part_ref.at[step - 1],
            dst_ref=recv_ref.at[step - 1],
            send_sem=part_send.at[step - 1],
            recv_sem=part_recv.at[step - 1],
            device_id={"seg": lax.rem(seg + step, n_seg)},
            device_id_type=MESH,
        )

    half = (n_seg + 1) // 2
    result = None
    for steps in (list(range(half, n_seg)), list(range(1, half)) + [0]):
        sums = fine_blocks([lax.rem(seg + step, n_seg) for step in steps])
        for step, block in zip(steps, sums):
            if step == 0:
                result = block
            else:
                part_ref[step - 1] = block
        for step in steps:
            if step > 0:
                part_copy(step).start()
    for step in range(1, n_seg):
        part_copy(step).wait_recv()
        result = result + recv_ref[step - 1]
    out_ref[...] = result
    for step in range(1, n_seg):
        part_copy(step).wait_send()
    for side, there in enumerate((has_up, has_down)):

        @pl.when(there)
        def _():
            edge_copy(side).wait_send()


def solution(mesh):
    n_seg = mesh.shape["seg"]
    n_band = mesh.shape["band"]
    placed = (
        P("seg", None, None, "band"),
        P("seg", None),
        P("seg", None, None, None),
        P("seg", None),
        P("seg", None),
        P(),
    )

    def per_device(sft, doppler, antenna, coarse_index, freq_offset, wing_width):
        segs_here, dets, _, bins = sft.shape
        fine = coarse_index.shape[1]
        own = fine // n_seg
        lines = segs_here * dets * 2
        operands = [
            pltpu.with_memory_space_constraint(operand, pltpu.HBM)
            for operand in (sft, doppler, antenna, coarse_index, freq_offset, wing_width)
        ]
        vmem = pl.BlockSpec(memory_space=pltpu.VMEM)
        hbm = pl.BlockSpec(memory_space=pltpu.HBM)
        return pl.pallas_call(
            functools.partial(kernel, n_seg, n_band, 0.25 / (segs_here * n_seg)),
            out_shape=jax.ShapeDtypeStruct((own, bins), jnp.float32),
            in_specs=[hbm] * 6,
            out_specs=vmem,
            scratch_shapes=[
                pltpu.VMEM(sft.shape, sft.dtype),
                pltpu.VMEM(doppler.shape, doppler.dtype),
                pltpu.VMEM(antenna.shape, antenna.dtype),
                pltpu.VMEM(coarse_index.shape, coarse_index.dtype),
                pltpu.VMEM(freq_offset.shape, freq_offset.dtype),
                pltpu.SMEM(wing_width.shape, wing_width.dtype),
                pltpu.VMEM((lines, bins), jnp.float32),
                pltpu.VMEM((2, lines, LANES), jnp.float32),
                pltpu.VMEM((ROWS * segs_here, doppler.shape[1]), jnp.float32),
                pltpu.VMEM((LANES, fine), jnp.float32),
                pltpu.VMEM((fine, LANES), jnp.float32),
                pltpu.VMEM((segs_here, 8, fine, 4 * (WMAX + OMAX) * dets), jnp.bfloat16),
                pltpu.VMEM((n_seg - 1, own, bins), jnp.float32),
                pltpu.VMEM((n_seg - 1, own, bins), jnp.float32),
                pltpu.SemaphoreType.DMA((6,)),
                pltpu.SemaphoreType.DMA((2,)),
                pltpu.SemaphoreType.DMA((2,)),
                pltpu.SemaphoreType.DMA((n_seg - 1,)),
                pltpu.SemaphoreType.DMA((n_seg - 1,)),
            ],
            compiler_params=pltpu.CompilerParams(
                collective_id=0, has_side_effects=True, vmem_limit_bytes=40 * 1024 * 1024
            ),
        )(*operands)

    return jax.shard_map(
        per_device, mesh=mesh, in_specs=placed, out_specs=P("seg", "band"), check_vma=False
    )
```

```python
import functools
import math

import jax
import jax.numpy as jnp
from jax import lax
from jax.experimental import pallas as pl
from jax.experimental.pallas import tpu as pltpu
from jax.sharding import PartitionSpec as P

WMAX = 32
OMAX = 32
LANES = 128
ROWS = 8
MESH = pl.DeviceIdType.MESH


def half_turn(x):
    rest = x - jnp.round(x)
    angle = rest * math.pi
    square = angle * angle
    sine = jnp.zeros_like(x)
    cosine = jnp.zeros_like(x)
    for power in range(7, -1, -1):
        sign = -1.0 if power % 2 else 1.0
        cosine = cosine * square + sign / math.factorial(2 * power)
        sine = sine * square + sign / math.factorial(2 * power + 1)
    return sine * angle, cosine


def gathered_rows(rows, indices):
    first = rows.astype(jnp.bfloat16).astype(jnp.float32)
    rest = rows - first
    second = rest.astype(jnp.bfloat16).astype(jnp.float32)
    third = rest - second
    parts = jnp.concatenate([first, second, third, jnp.zeros_like(first)], axis=0)
    places = lax.broadcasted_iota(jnp.int32, (rows.shape[1], indices.shape[1]), 0)
    chosen = jnp.where(places == indices, 1.0, 0.0).astype(jnp.bfloat16)
    picked = jnp.dot(parts.astype(jnp.bfloat16), chosen, preferred_element_type=jnp.float32)
    count = rows.shape[0]
    return picked[:count] + picked[count : 2 * count] + picked[2 * count : 3 * count]


def kernel(
    n_seg,
    n_band,
    scale,
    sft_hbm,
    doppler_hbm,
    antenna_hbm,
    index_hbm,
    offset_hbm,
    wing_hbm,
    out_ref,
    sft_ref,
    doppler_ref,
    antenna_ref,
    index_ref,
    offset_ref,
    wing_ref,
    param_ref,
    fine_ref,
    column_ref,
    x_ref,
    edge_ref,
    block_ref,
    unfolded_ref,
    load_sem,
    x_send,
    x_recv,
    edge_send,
    edge_recv,
    block_send,
    block_recv,
):
    seg = lax.axis_index("seg")
    band = lax.axis_index("band")
    segs_here, dets, _, bins = sft_ref.shape
    fine = index_ref.shape[1]
    own = fine // n_seg
    lines = 2 * dets
    has_up = band < n_band - 1
    has_down = band > 0
    up = jnp.minimum(band + 1, n_band - 1)
    down = jnp.maximum(band - 1, 0)
    peers = [lax.rem(seg + step, n_seg) for step in range(n_seg)]

    barrier = pltpu.get_barrier_semaphore()

    def greet(peer, there):
        pl.semaphore_signal(
            barrier, inc=1, device_id={"seg": peer, "band": there}, device_id_type=MESH
        )

    for peer in peers[1:]:
        greet(peer, band)
    for there, neighbour in ((has_up, up), (has_down, down)):

        @pl.when(there)
        def _():
            for peer in peers:
                greet(peer, neighbour)

    loads = []
    for source, target in (
        (sft_hbm, sft_ref),
        (doppler_hbm, doppler_ref),
        (antenna_hbm, antenna_ref),
        (index_hbm, index_ref),
        (offset_hbm, offset_ref),
        (wing_hbm, wing_ref),
    ):
        loads.append(pltpu.make_async_copy(source, target, load_sem.at[len(loads)]))
        loads[-1].start()
    loads[0].wait()
    for s in range(segs_here):
        for d in range(dets):
            first = s * lines + 2 * d
            x_ref[0, first : first + 2, :] = sft_ref[s, d].astype(jnp.float32)
    sides = has_up.astype(jnp.int32) + has_down.astype(jnp.int32)
    pl.semaphore_wait(barrier, n_seg - 1 + n_seg * sides)

    def edge_copy(side, step):
        start, neighbour = ((bins - LANES, up), (0, down))[side]
        return pltpu.make_async_remote_copy(
            src_ref=x_ref.at[0, :, pl.ds(start, LANES)],
            dst_ref=edge_ref.at[step, side],
            send_sem=edge_send.at[side, step],
            recv_sem=edge_recv.at[side, step],
            device_id={"seg": peers[step], "band": neighbour},
            device_id_type=MESH,
        )

    def x_copy(step):
        return pltpu.make_async_remote_copy(
            src_ref=x_ref.at[0],
            dst_ref=x_ref.at[step],
            send_sem=x_send.at[step - 1],
            recv_sem=x_recv.at[step - 1],
            device_id={"seg": peers[step], "band": band},
            device_id_type=MESH,
        )

    def block_copy(step):
        return pltpu.make_async_remote_copy(
            src_ref=column_ref.at[pl.ds(pl.multiple_of(peers[step] * own, own), own)],
            dst_ref=block_ref.at[step - 1],
            send_sem=block_send.at[step - 1],
            recv_sem=block_recv.at[step - 1],
            device_id={"seg": peers[step], "band": band},
            device_id_type=MESH,
        )

    for side, there in enumerate((has_up, has_down)):

        @pl.when(there)
        def _():
            for step in range(n_seg):
                edge_copy(side, step).start()

    for step in range(1, n_seg):
        x_copy(step).start()

    for load in loads[1:]:
        load.wait()
    param_ref[...] = jnp.zeros_like(param_ref)
    fine_ref[...] = jnp.zeros_like(fine_ref)
    for s in range(segs_here):
        param_ref[ROWS * s : ROWS * s + 1, :] = doppler_ref[s : s + 1, :]
        for q in range(2):
            first = ROWS * s + 1 + dets * q
            param_ref[first : first + dets, :] = antenna_ref[s, q]
    for s in range(segs_here):
        rows = gathered_rows(param_ref[ROWS * s : ROWS * (s + 1), :], index_ref[s : s + 1, :])
        fine_ref[ROWS * s : ROWS * (s + 1), :] = rows
        sine, cosine = half_turn(rows[0:1])
        fine_ref[ROWS * s + 5 : ROWS * s + 6, :] = offset_ref[s : s + 1, :].astype(jnp.float32)
        fine_ref[ROWS * s + 6 : ROWS * s + 7, :] = sine
        fine_ref[ROWS * s + 7 : ROWS * s + 8, :] = cosine
    column_ref[...] = jnp.transpose(fine_ref[...])
    for step in range(1, n_seg):
        block_copy(step).start()

    span = 2 * (WMAX + OMAX)
    width = bins + span
    wing_low = jnp.where(has_down, wing_ref[down], 0).astype(jnp.float32)
    wing_mid = wing_ref[band].astype(jnp.float32)
    wing_high = jnp.where(has_up, wing_ref[up], 0).astype(jnp.float32)
    lane = lax.broadcasted_iota(jnp.int32, (own, span), 1)
    reach = (span // 2 - 1 - lane).astype(jnp.float32)
    place = lax.broadcasted_iota(jnp.int32, (own, bins), 1).astype(jnp.float32)

    def demodulators(columns, s):
        column = lambda row: columns[:, ROWS * s + row : ROWS * s + row + 1]
        offset = column(5)
        tap = reach - offset
        u = tap - column(0)
        centre = u == 0.0
        envelope = jnp.where(
            centre, 1.0, -column(6) / jnp.where(centre, 1.0, math.pi * u)
        )
        real_part = envelope * column(7)
        imag_part = envelope * column(6)
        blocks = []
        for wing in (wing_mid, jnp.where(offset < 0.0, wing_low, wing_high)):
            inside = (tap >= -wing) & (tap < wing)
            real = jnp.where(inside, real_part, 0.0)
            imag = jnp.where(inside, imag_part, 0.0)
            for q in range(2):
                to_real, to_imag = [], []
                for d in range(dets):
                    weight = column(1 + dets * q + d)
                    weighted_real = (weight * real).astype(jnp.bfloat16)
                    weighted_imag = (weight * imag).astype(jnp.bfloat16)
                    to_real += [weighted_real, -weighted_imag]
                    to_imag += [weighted_imag, weighted_real]
                blocks.append(jnp.concatenate(to_real, axis=1))
                blocks.append(jnp.concatenate(to_imag, axis=1))
        return jnp.concatenate(blocks, axis=0)

    def unfold(low, middle, high):
        padded = jnp.concatenate(
            [jnp.where(has_down, low, 0.0), middle, jnp.where(has_up, high, 0.0)], axis=1
        )
        margin = LANES - WMAX - OMAX
        padded = pltpu.roll(padded, padded.shape[1] - margin, 1)[:, :width]
        spreads = []
        for line in range(segs_here * lines):
            spread = jnp.broadcast_to(padded[line : line + 1, :], (span, width))
            spread = pltpu.roll(spread, width - span + 1, 1, stride=1, stride_axis=0)
            spreads.append(spread[:, :bins].astype(jnp.bfloat16))
        return [
            jnp.concatenate(spreads[s * lines : (s + 1) * lines], axis=0)
            for s in range(segs_here)
        ]

    def moved_coarse(columns, s, kernels, unfolded):
        amplitude = jnp.dot(kernels, unfolded, preferred_element_type=jnp.float32)
        power = amplitude * amplitude
        parts = [power[own * part : own * (part + 1)] for part in range(8)]
        middle = (parts[0] + parts[1]) + (parts[2] + parts[3])
        beside = (parts[4] + parts[5]) + (parts[6] + parts[7])
        there = place + columns[:, ROWS * s + 5 : ROWS * s + 6]
        return jnp.where((there >= 0.0) & (there < float(bins)), middle, beside)

    def wait_edges(step):
        for side, there in enumerate((has_down, has_up)):

            @pl.when(there)
            def _():
                edge_copy(side, step).wait_recv()

    wait_edges(0)
    columns = column_ref[pl.ds(pl.multiple_of(seg * own, own), own), :]
    unfolded = unfold(edge_ref[0, 0], x_ref[0], edge_ref[0, 1])
    total = None
    for s in range(segs_here):
        term = moved_coarse(columns, s, demodulators(columns, s), unfolded[s])
        total = term if total is None else total + term
    for step in range(1, n_seg):
        wait_edges(step)
        x_copy(step).wait_recv()
    for step in range(1, n_seg):
        unfolded = unfold(edge_ref[step, 0], x_ref[step], edge_ref[step, 1])
        for s in range(segs_here):
            unfolded_ref[step - 1, s] = unfolded[s]
    for step in range(1, n_seg):
        block_copy(step).wait_recv()
    for step in range(1, n_seg):
        columns = block_ref[step - 1]
        for s in range(segs_here):
            kernels = demodulators(columns, s)
            total = total + moved_coarse(columns, s, kernels, unfolded_ref[step - 1, s])
    out_ref[...] = total * scale

    for step in range(1, n_seg):
        x_copy(step).wait_send()
        block_copy(step).wait_send()
    for side, there in enumerate((has_up, has_down)):

        @pl.when(there)
        def _():
            for step in range(n_seg):
                edge_copy(side, step).wait_send()


def solution(mesh):
    n_seg = mesh.shape["seg"]
    n_band = mesh.shape["band"]
    placed = (
        P("seg", None, None, "band"),
        P("seg", None),
        P("seg", None, None, None),
        P("seg", None),
        P("seg", None),
        P(),
    )

    def per_device(sft, doppler, antenna, coarse_index, freq_offset, wing_width):
        segs_here, dets, _, bins = sft.shape
        fine = coarse_index.shape[1]
        own = fine // n_seg
        lines = segs_here * dets * 2
        operands = [
            pltpu.with_memory_space_constraint(operand, pltpu.HBM)
            for operand in (sft, doppler, antenna, coarse_index, freq_offset, wing_width)
        ]
        vmem = pl.BlockSpec(memory_space=pltpu.VMEM)
        hbm = pl.BlockSpec(memory_space=pltpu.HBM)
        return pl.pallas_call(
            functools.partial(kernel, n_seg, n_band, 0.25 / (segs_here * n_seg)),
            out_shape=jax.ShapeDtypeStruct((own, bins), jnp.float32),
            in_specs=[hbm] * 6,
            out_specs=vmem,
            scratch_shapes=[
                pltpu.VMEM(sft.shape, sft.dtype),
                pltpu.VMEM(doppler.shape, doppler.dtype),
                pltpu.VMEM(antenna.shape, antenna.dtype),
                pltpu.VMEM(coarse_index.shape, coarse_index.dtype),
                pltpu.VMEM(freq_offset.shape, freq_offset.dtype),
                pltpu.SMEM(wing_width.shape, wing_width.dtype),
                pltpu.VMEM((ROWS * segs_here, doppler.shape[1]), jnp.float32),
                pltpu.VMEM((LANES, fine), jnp.float32),
                pltpu.VMEM((fine, LANES), jnp.float32),
                pltpu.VMEM((n_seg, lines, bins), jnp.float32),
                pltpu.VMEM((n_seg, 2, lines, LANES), jnp.float32),
                pltpu.VMEM((n_seg - 1, own, LANES), jnp.float32),
                pltpu.VMEM(
                    (n_seg - 1, segs_here, 4 * (WMAX + OMAX) * dets, bins), jnp.bfloat16
                ),
                pltpu.SemaphoreType.DMA((6,)),
                pltpu.SemaphoreType.DMA((n_seg - 1,)),
                pltpu.SemaphoreType.DMA((n_seg - 1,)),
                pltpu.SemaphoreType.DMA((2, n_seg)),
                pltpu.SemaphoreType.DMA((2, n_seg)),
                pltpu.SemaphoreType.DMA((n_seg - 1,)),
                pltpu.SemaphoreType.DMA((n_seg - 1,)),
            ],
            compiler_params=pltpu.CompilerParams(
                collective_id=0, has_side_effects=True, vmem_limit_bytes=40 * 1024 * 1024
            ),
        )(*operands)

    return jax.shard_map(
        per_device, mesh=mesh, in_specs=placed, out_specs=P("seg", "band"), check_vma=False
    )
```

```python
import functools
import math

import jax
import jax.numpy as jnp
from jax import lax
from jax.experimental import pallas as pl
from jax.experimental.pallas import tpu as pltpu
from jax.sharding import PartitionSpec as P

WMAX = 32
OMAX = 32
LANES = 128
ROWS = 8
MESH = pl.DeviceIdType.MESH


def half_turn(x):
    rest = x - jnp.round(x)
    angle = rest * math.pi
    square = angle * angle
    sine = jnp.zeros_like(x)
    cosine = jnp.zeros_like(x)
    for power in range(7, -1, -1):
        sign = -1.0 if power % 2 else 1.0
        cosine = cosine * square + sign / math.factorial(2 * power)
        sine = sine * square + sign / math.factorial(2 * power + 1)
    return sine * angle, cosine


def gathered_rows(rows, indices):
    first = rows.astype(jnp.bfloat16).astype(jnp.float32)
    rest = rows - first
    second = rest.astype(jnp.bfloat16).astype(jnp.float32)
    third = rest - second
    parts = jnp.concatenate([first, second, third, jnp.zeros_like(first)], axis=0)
    places = lax.broadcasted_iota(jnp.int32, (rows.shape[1], indices.shape[1]), 0)
    chosen = jnp.where(places == indices, 1.0, 0.0).astype(jnp.bfloat16)
    picked = jnp.dot(parts.astype(jnp.bfloat16), chosen, preferred_element_type=jnp.float32)
    count = rows.shape[0]
    return picked[:count] + picked[count : 2 * count] + picked[2 * count : 3 * count]


def kernel(
    n_seg,
    n_band,
    scale,
    sft_hbm,
    doppler_hbm,
    antenna_hbm,
    index_hbm,
    offset_hbm,
    wing_hbm,
    out_ref,
    sft_ref,
    doppler_ref,
    antenna_ref,
    index_ref,
    offset_ref,
    wing_ref,
    param_ref,
    fine_ref,
    column_ref,
    x_ref,
    edge_ref,
    block_ref,
    load_sem,
    x_send,
    x_recv,
    edge_send,
    edge_recv,
    block_send,
    block_recv,
):
    seg = lax.axis_index("seg")
    band = lax.axis_index("band")
    segs_here, dets, _, bins = sft_ref.shape
    fine = index_ref.shape[1]
    own = fine // n_seg
    lines = 2 * dets
    has_up = band < n_band - 1
    has_down = band > 0
    up = jnp.minimum(band + 1, n_band - 1)
    down = jnp.maximum(band - 1, 0)
    peers = [lax.rem(seg + step, n_seg) for step in range(n_seg)]

    barrier = pltpu.get_barrier_semaphore()

    def greet(peer, there):
        pl.semaphore_signal(
            barrier, inc=1, device_id={"seg": peer, "band": there}, device_id_type=MESH
        )

    for peer in peers[1:]:
        greet(peer, band)
    for there, neighbour in ((has_up, up), (has_down, down)):

        @pl.when(there)
        def _():
            for peer in peers:
                greet(peer, neighbour)

    loads = []
    for source, target in (
        (sft_hbm, sft_ref),
        (doppler_hbm, doppler_ref),
        (antenna_hbm, antenna_ref),
        (index_hbm, index_ref),
        (offset_hbm, offset_ref),
        (wing_hbm, wing_ref),
    ):
        loads.append(pltpu.make_async_copy(source, target, load_sem.at[len(loads)]))
        loads[-1].start()
    loads[0].wait()
    for s in range(segs_here):
        for d in range(dets):
            first = s * lines + 2 * d
            x_ref[0, first : first + 2, :] = sft_ref[s, d].astype(jnp.float32)
    for load in loads[1:]:
        load.wait()
    param_ref[...] = jnp.zeros_like(param_ref)
    fine_ref[...] = jnp.zeros_like(fine_ref)
    for s in range(segs_here):
        param_ref[ROWS * s : ROWS * s + 1, :] = doppler_ref[s : s + 1, :]
        for q in range(2):
            first = ROWS * s + 1 + dets * q
            param_ref[first : first + dets, :] = antenna_ref[s, q]
    for s in range(segs_here):
        rows = gathered_rows(param_ref[ROWS * s : ROWS * (s + 1), :], index_ref[s : s + 1, :])
        fine_ref[ROWS * s : ROWS * (s + 1), :] = rows
        sine, cosine = half_turn(rows[0:1])
        fine_ref[ROWS * s + 5 : ROWS * s + 6, :] = offset_ref[s : s + 1, :].astype(jnp.float32)
        fine_ref[ROWS * s + 6 : ROWS * s + 7, :] = sine
        fine_ref[ROWS * s + 7 : ROWS * s + 8, :] = cosine
    column_ref[...] = jnp.transpose(fine_ref[...])
    sides = has_up.astype(jnp.int32) + has_down.astype(jnp.int32)
    pl.semaphore_wait(barrier, n_seg - 1 + n_seg * sides)

    def edge_copy(side, step):
        start, neighbour = ((bins - LANES, up), (0, down))[side]
        return pltpu.make_async_remote_copy(
            src_ref=x_ref.at[0, :, pl.ds(start, LANES)],
            dst_ref=edge_ref.at[step, side],
            send_sem=edge_send.at[side, step],
            recv_sem=edge_recv.at[side, step],
            device_id={"seg": peers[step], "band": neighbour},
            device_id_type=MESH,
        )

    def x_copy(step):
        return pltpu.make_async_remote_copy(
            src_ref=x_ref.at[0],
            dst_ref=x_ref.at[step],
            send_sem=x_send.at[step - 1],
            recv_sem=x_recv.at[step - 1],
            device_id={"seg": peers[step], "band": band},
            device_id_type=MESH,
        )

    def block_copy(step):
        return pltpu.make_async_remote_copy(
            src_ref=column_ref.at[pl.ds(pl.multiple_of(peers[step] * own, own), own)],
            dst_ref=block_ref.at[step - 1],
            send_sem=block_send.at[step - 1],
            recv_sem=block_recv.at[step - 1],
            device_id={"seg": peers[step], "band": band},
            device_id_type=MESH,
        )

    for side, there in enumerate((has_up, has_down)):

        @pl.when(there)
        def _():
            for step in range(n_seg):
                edge_copy(side, step).start()

    for step in range(1, n_seg):
        x_copy(step).start()

    for step in range(1, n_seg):
        block_copy(step).start()

    span = 2 * (WMAX + OMAX)
    width = bins + span
    wing_low = jnp.where(has_down, wing_ref[down], 0).astype(jnp.float32)
    wing_mid = wing_ref[band].astype(jnp.float32)
    wing_high = jnp.where(has_up, wing_ref[up], 0).astype(jnp.float32)
    lane = lax.broadcasted_iota(jnp.int32, (own, span), 1)
    reach = (span // 2 - 1 - lane).astype(jnp.float32)
    place = lax.broadcasted_iota(jnp.int32, (own, bins), 1).astype(jnp.float32)

    def demodulators(columns, s):
        column = lambda row: columns[:, ROWS * s + row : ROWS * s + row + 1]
        offset = column(5)
        tap = reach - offset
        u = tap - column(0)
        centre = u == 0.0
        envelope = jnp.where(
            centre, 1.0, -column(6) / jnp.where(centre, 1.0, math.pi * u)
        )
        real_part = envelope * column(7)
        imag_part = envelope * column(6)
        blocks = []
        for wing in (wing_mid, jnp.where(offset < 0.0, wing_low, wing_high)):
            inside = (tap >= -wing) & (tap < wing)
            real = jnp.where(inside, real_part, 0.0)
            imag = jnp.where(inside, imag_part, 0.0)
            for q in range(2):
                to_real, to_imag = [], []
                for d in range(dets):
                    weight = column(1 + dets * q + d)
                    weighted_real = (weight * real).astype(jnp.bfloat16)
                    weighted_imag = (weight * imag).astype(jnp.bfloat16)
                    to_real += [weighted_real, -weighted_imag]
                    to_imag += [weighted_imag, weighted_real]
                blocks.append(jnp.concatenate(to_real, axis=1))
                blocks.append(jnp.concatenate(to_imag, axis=1))
        return jnp.concatenate(blocks, axis=0)

    def unfold(low, middle, high):
        padded = jnp.concatenate(
            [jnp.where(has_down, low, 0.0), middle, jnp.where(has_up, high, 0.0)], axis=1
        )
        margin = LANES - WMAX - OMAX
        tile_lane = lax.broadcasted_iota(jnp.int32, (ROWS, LANES), 1)
        padded = pltpu.roll(padded, padded.shape[1] - margin, 1)[:, :width]
        spreads = []
        for line in range(segs_here * lines):
            rows = jnp.broadcast_to(padded[line : line + 1, :], (ROWS, width))
            rows = pltpu.roll(rows, 0, 1, stride=1, stride_axis=0)
            tiles = [rows[:, at : at + LANES] for at in range(0, width, LANES)]
            pieces = []
            for first in range(0, span, ROWS):
                back = LANES - (span - 1 - first)
                turned = [pltpu.roll(tile, back, 1) for tile in tiles]
                chosen = [
                    jnp.where(tile_lane < back, turned[at], turned[at + 1])
                    for at in range(bins // LANES)
                ]
                pieces.append(jnp.concatenate(chosen, axis=1))
            spreads.append(jnp.concatenate(pieces, axis=0).astype(jnp.bfloat16))
        return [
            jnp.concatenate(spreads[s * lines : (s + 1) * lines], axis=0)
            for s in range(segs_here)
        ]

    def moved_coarse(columns, s, kernels, unfolded):
        amplitude = jnp.dot(kernels, unfolded, preferred_element_type=jnp.float32)
        power = amplitude * amplitude
        parts = [power[own * part : own * (part + 1)] for part in range(8)]
        middle = (parts[0] + parts[1]) + (parts[2] + parts[3])
        beside = (parts[4] + parts[5]) + (parts[6] + parts[7])
        there = place + columns[:, ROWS * s + 5 : ROWS * s + 6]
        return jnp.where((there >= 0.0) & (there < float(bins)), middle, beside)

    def segment_sum(columns, x_slot):
        unfolded = unfold(edge_ref[x_slot, 0], x_ref[x_slot], edge_ref[x_slot, 1])
        result = None
        for s in range(segs_here):
            term = moved_coarse(columns, s, demodulators(columns, s), unfolded[s])
            result = term if result is None else result + term
        return result

    def wait_edges(step):
        for side, there in enumerate((has_down, has_up)):

            @pl.when(there)
            def _():
                edge_copy(side, step).wait_recv()

    wait_edges(0)
    columns = column_ref[pl.ds(pl.multiple_of(seg * own, own), own), :]
    total = segment_sum(columns, 0)
    for step in range(1, n_seg):
        wait_edges(step)
        x_copy(step).wait_recv()
        block_copy(step).wait_recv()
    for step in range(1, n_seg):
        total = total + segment_sum(block_ref[step - 1], step)
    out_ref[...] = total * scale

    for step in range(1, n_seg):
        x_copy(step).wait_send()
        block_copy(step).wait_send()
    for side, there in enumerate((has_up, has_down)):

        @pl.when(there)
        def _():
            for step in range(n_seg):
                edge_copy(side, step).wait_send()


def solution(mesh):
    n_seg = mesh.shape["seg"]
    n_band = mesh.shape["band"]
    placed = (
        P("seg", None, None, "band"),
        P("seg", None),
        P("seg", None, None, None),
        P("seg", None),
        P("seg", None),
        P(),
    )

    def per_device(sft, doppler, antenna, coarse_index, freq_offset, wing_width):
        segs_here, dets, _, bins = sft.shape
        fine = coarse_index.shape[1]
        own = fine // n_seg
        lines = segs_here * dets * 2
        operands = [
            pltpu.with_memory_space_constraint(operand, pltpu.HBM)
            for operand in (sft, doppler, antenna, coarse_index, freq_offset, wing_width)
        ]
        vmem = pl.BlockSpec(memory_space=pltpu.VMEM)
        hbm = pl.BlockSpec(memory_space=pltpu.HBM)
        return pl.pallas_call(
            functools.partial(kernel, n_seg, n_band, 0.25 / (segs_here * n_seg)),
            out_shape=jax.ShapeDtypeStruct((own, bins), jnp.float32),
            in_specs=[hbm] * 6,
            out_specs=vmem,
            scratch_shapes=[
                pltpu.VMEM(sft.shape, sft.dtype),
                pltpu.VMEM(doppler.shape, doppler.dtype),
                pltpu.VMEM(antenna.shape, antenna.dtype),
                pltpu.VMEM(coarse_index.shape, coarse_index.dtype),
                pltpu.VMEM(freq_offset.shape, freq_offset.dtype),
                pltpu.SMEM(wing_width.shape, wing_width.dtype),
                pltpu.VMEM((ROWS * segs_here, doppler.shape[1]), jnp.float32),
                pltpu.VMEM((LANES, fine), jnp.float32),
                pltpu.VMEM((fine, LANES), jnp.float32),
                pltpu.VMEM((n_seg, lines, bins), jnp.float32),
                pltpu.VMEM((n_seg, 2, lines, LANES), jnp.float32),
                pltpu.VMEM((n_seg - 1, own, LANES), jnp.float32),
                pltpu.SemaphoreType.DMA((6,)),
                pltpu.SemaphoreType.DMA((n_seg - 1,)),
                pltpu.SemaphoreType.DMA((n_seg - 1,)),
                pltpu.SemaphoreType.DMA((2, n_seg)),
                pltpu.SemaphoreType.DMA((2, n_seg)),
                pltpu.SemaphoreType.DMA((n_seg - 1,)),
                pltpu.SemaphoreType.DMA((n_seg - 1,)),
            ],
            compiler_params=pltpu.CompilerParams(
                collective_id=0, has_side_effects=True, vmem_limit_bytes=40 * 1024 * 1024
            ),
        )(*operands)

    return jax.shard_map(
        per_device, mesh=mesh, in_specs=placed, out_specs=P("seg", "band"), check_vma=False
    )
```

```python
import functools
import math

import jax
import jax.numpy as jnp
from jax import lax
from jax.experimental import pallas as pl
from jax.experimental.pallas import tpu as pltpu
from jax.sharding import PartitionSpec as P

WMAX = 32
OMAX = 32
LANES = 128
ROWS = 8
MESH = pl.DeviceIdType.MESH


def half_turn(x):
    rest = x - jnp.round(x)
    angle = rest * math.pi
    square = angle * angle
    sine = jnp.zeros_like(x)
    cosine = jnp.zeros_like(x)
    for power in range(7, -1, -1):
        sign = -1.0 if power % 2 else 1.0
        cosine = cosine * square + sign / math.factorial(2 * power)
        sine = sine * square + sign / math.factorial(2 * power + 1)
    return sine * angle, cosine


def gathered_rows(rows, indices):
    first = rows.astype(jnp.bfloat16).astype(jnp.float32)
    rest = rows - first
    second = rest.astype(jnp.bfloat16).astype(jnp.float32)
    third = rest - second
    parts = jnp.concatenate([first, second, third, jnp.zeros_like(first)], axis=0)
    places = lax.broadcasted_iota(jnp.int32, (rows.shape[1], indices.shape[1]), 0)
    chosen = jnp.where(places == indices, 1.0, 0.0).astype(jnp.bfloat16)
    picked = jnp.dot(parts.astype(jnp.bfloat16), chosen, preferred_element_type=jnp.float32)
    count = rows.shape[0]
    return picked[:count] + picked[count : 2 * count] + picked[2 * count : 3 * count]


def kernel(
    n_seg,
    n_band,
    scale,
    sft_hbm,
    doppler_hbm,
    antenna_hbm,
    index_hbm,
    offset_hbm,
    wing_hbm,
    out_ref,
    sft_ref,
    doppler_ref,
    antenna_ref,
    index_ref,
    offset_ref,
    wing_ref,
    param_ref,
    fine_ref,
    column_ref,
    x_ref,
    edge_ref,
    block_ref,
    load_sem,
    x_send,
    x_recv,
    edge_send,
    edge_recv,
    block_send,
    block_recv,
):
    seg = lax.axis_index("seg")
    band = lax.axis_index("band")
    segs_here, dets, _, bins = sft_ref.shape
    fine = index_ref.shape[1]
    own = fine // n_seg
    lines = 2 * dets
    has_up = band < n_band - 1
    has_down = band > 0
    up = jnp.minimum(band + 1, n_band - 1)
    down = jnp.maximum(band - 1, 0)
    peers = [lax.rem(seg + step, n_seg) for step in range(n_seg)]

    barrier = pltpu.get_barrier_semaphore()

    def greet(peer, there):
        pl.semaphore_signal(
            barrier, inc=1, device_id={"seg": peer, "band": there}, device_id_type=MESH
        )

    for peer in peers[1:]:
        greet(peer, band)
    for there, neighbour in ((has_up, up), (has_down, down)):

        @pl.when(there)
        def _():
            for peer in peers:
                greet(peer, neighbour)

    loads = []
    for source, target in (
        (sft_hbm, sft_ref),
        (doppler_hbm, doppler_ref),
        (antenna_hbm, antenna_ref),
        (index_hbm, index_ref),
        (offset_hbm, offset_ref),
        (wing_hbm, wing_ref),
    ):
        loads.append(pltpu.make_async_copy(source, target, load_sem.at[len(loads)]))
        loads[-1].start()
    loads[0].wait()
    for s in range(segs_here):
        for d in range(dets):
            first = s * lines + 2 * d
            x_ref[0, first : first + 2, :] = sft_ref[s, d].astype(jnp.float32)
    for load in loads[1:]:
        load.wait()
    param_ref[...] = jnp.zeros_like(param_ref)
    fine_ref[...] = jnp.zeros_like(fine_ref)
    for s in range(segs_here):
        param_ref[ROWS * s : ROWS * s + 1, :] = doppler_ref[s : s + 1, :]
        for q in range(2):
            first = ROWS * s + 1 + dets * q
            param_ref[first : first + dets, :] = antenna_ref[s, q]
    for s in range(segs_here):
        rows = gathered_rows(param_ref[ROWS * s : ROWS * (s + 1), :], index_ref[s : s + 1, :])
        fine_ref[ROWS * s : ROWS * (s + 1), :] = rows
        sine, cosine = half_turn(rows[0:1])
        fine_ref[ROWS * s + 5 : ROWS * s + 6, :] = offset_ref[s : s + 1, :].astype(jnp.float32)
        fine_ref[ROWS * s + 6 : ROWS * s + 7, :] = sine
        fine_ref[ROWS * s + 7 : ROWS * s + 8, :] = cosine
    column_ref[...] = jnp.transpose(fine_ref[...])
    sides = has_up.astype(jnp.int32) + has_down.astype(jnp.int32)
    pl.semaphore_wait(barrier, n_seg - 1 + n_seg * sides)

    def edge_copy(side, step):
        start, neighbour = ((bins - LANES, up), (0, down))[side]
        return pltpu.make_async_remote_copy(
            src_ref=x_ref.at[0, :, pl.ds(start, LANES)],
            dst_ref=edge_ref.at[step, side],
            send_sem=edge_send.at[side, step],
            recv_sem=edge_recv.at[side, step],
            device_id={"seg": peers[step], "band": neighbour},
            device_id_type=MESH,
        )

    def x_copy(step):
        return pltpu.make_async_remote_copy(
            src_ref=x_ref.at[0],
            dst_ref=x_ref.at[step],
            send_sem=x_send.at[step - 1],
            recv_sem=x_recv.at[step - 1],
            device_id={"seg": peers[step], "band": band},
            device_id_type=MESH,
        )

    def block_copy(step):
        return pltpu.make_async_remote_copy(
            src_ref=column_ref.at[pl.ds(pl.multiple_of(peers[step] * own, own), own)],
            dst_ref=block_ref.at[step - 1],
            send_sem=block_send.at[step - 1],
            recv_sem=block_recv.at[step - 1],
            device_id={"seg": peers[step], "band": band},
            device_id_type=MESH,
        )

    for side, there in enumerate((has_up, has_down)):

        @pl.when(there)
        def _():
            for step in range(n_seg):
                edge_copy(side, step).start()

    for step in range(1, n_seg):
        x_copy(step).start()

    for step in range(1, n_seg):
        block_copy(step).start()

    span = 2 * (WMAX + OMAX)
    width = bins + span
    wing_low = jnp.where(has_down, wing_ref[down], 0).astype(jnp.float32)
    wing_mid = wing_ref[band].astype(jnp.float32)
    wing_high = jnp.where(has_up, wing_ref[up], 0).astype(jnp.float32)
    lane = lax.broadcasted_iota(jnp.int32, (own, span), 1)
    reach = (span // 2 - 1 - lane).astype(jnp.float32)
    place = lax.broadcasted_iota(jnp.int32, (own, bins), 1).astype(jnp.float32)

    def demodulators(columns, s):
        column = lambda row: columns[:, ROWS * s + row : ROWS * s + row + 1]
        offset = column(5)
        tap = reach - offset
        u = tap - column(0)
        centre = u == 0.0
        envelope = jnp.where(
            centre, 1.0, -column(6) / jnp.where(centre, 1.0, math.pi * u)
        )
        real_part = envelope * column(7)
        imag_part = envelope * column(6)
        blocks = []
        for wing in (wing_mid, jnp.where(offset < 0.0, wing_low, wing_high)):
            inside = (tap >= -wing) & (tap < wing)
            real = jnp.where(inside, real_part, 0.0)
            imag = jnp.where(inside, imag_part, 0.0)
            for q in range(2):
                to_real, to_imag = [], []
                for d in range(dets):
                    weight = column(1 + dets * q + d)
                    weighted_real = (weight * real).astype(jnp.bfloat16)
                    weighted_imag = (weight * imag).astype(jnp.bfloat16)
                    to_real += [weighted_real, -weighted_imag]
                    to_imag += [weighted_imag, weighted_real]
                blocks.append(jnp.concatenate(to_real, axis=1))
                blocks.append(jnp.concatenate(to_imag, axis=1))
        return jnp.concatenate(blocks, axis=0)

    def unfold(low, middle, high):
        padded = jnp.concatenate(
            [jnp.where(has_down, low, 0.0), middle, jnp.where(has_up, high, 0.0)], axis=1
        )
        margin = LANES - WMAX - OMAX
        row_at = lax.broadcasted_iota(jnp.int32, (span, LANES), 0)
        this_tile = lax.broadcasted_iota(jnp.int32, (span, LANES), 1) <= row_at
        padded = pltpu.roll(padded, padded.shape[1] - margin, 1)[:, :width]
        spreads = []
        for line in range(segs_here * lines):
            turned = []
            for at in range(0, width, LANES):
                tile = jnp.broadcast_to(padded[line : line + 1, at : at + LANES], (span, LANES))
                turned.append(pltpu.roll(tile, LANES + 1 - span, 1, stride=1, stride_axis=0))
            chosen = [
                jnp.where(this_tile, turned[at], turned[at + 1]).astype(jnp.bfloat16)
                for at in range(bins // LANES)
            ]
            spreads.append(jnp.concatenate(chosen, axis=1))
        return [
            jnp.concatenate(spreads[s * lines : (s + 1) * lines], axis=0)
            for s in range(segs_here)
        ]

    def moved_coarse(columns, s, kernels, unfolded):
        amplitude = jnp.dot(kernels, unfolded, preferred_element_type=jnp.float32)
        power = amplitude * amplitude
        parts = [power[own * part : own * (part + 1)] for part in range(8)]
        middle = (parts[0] + parts[1]) + (parts[2] + parts[3])
        beside = (parts[4] + parts[5]) + (parts[6] + parts[7])
        there = place + columns[:, ROWS * s + 5 : ROWS * s + 6]
        return jnp.where((there >= 0.0) & (there < float(bins)), middle, beside)

    def segment_sum(columns, x_slot):
        unfolded = unfold(edge_ref[x_slot, 0], x_ref[x_slot], edge_ref[x_slot, 1])
        result = None
        for s in range(segs_here):
            term = moved_coarse(columns, s, demodulators(columns, s), unfolded[s])
            result = term if result is None else result + term
        return result

    def wait_edges(step):
        for side, there in enumerate((has_down, has_up)):

            @pl.when(there)
            def _():
                edge_copy(side, step).wait_recv()

    wait_edges(0)
    columns = column_ref[pl.ds(pl.multiple_of(seg * own, own), own), :]
    total = segment_sum(columns, 0)
    for step in range(1, n_seg):
        wait_edges(step)
        x_copy(step).wait_recv()
        block_copy(step).wait_recv()
    for step in range(1, n_seg):
        total = total + segment_sum(block_ref[step - 1], step)
    out_ref[...] = total * scale

    for step in range(1, n_seg):
        x_copy(step).wait_send()
        block_copy(step).wait_send()
    for side, there in enumerate((has_up, has_down)):

        @pl.when(there)
        def _():
            for step in range(n_seg):
                edge_copy(side, step).wait_send()


def solution(mesh):
    n_seg = mesh.shape["seg"]
    n_band = mesh.shape["band"]
    placed = (
        P("seg", None, None, "band"),
        P("seg", None),
        P("seg", None, None, None),
        P("seg", None),
        P("seg", None),
        P(),
    )

    def per_device(sft, doppler, antenna, coarse_index, freq_offset, wing_width):
        segs_here, dets, _, bins = sft.shape
        fine = coarse_index.shape[1]
        own = fine // n_seg
        lines = segs_here * dets * 2
        operands = [
            pltpu.with_memory_space_constraint(operand, pltpu.HBM)
            for operand in (sft, doppler, antenna, coarse_index, freq_offset, wing_width)
        ]
        vmem = pl.BlockSpec(memory_space=pltpu.VMEM)
        hbm = pl.BlockSpec(memory_space=pltpu.HBM)
        return pl.pallas_call(
            functools.partial(kernel, n_seg, n_band, 0.25 / (segs_here * n_seg)),
            out_shape=jax.ShapeDtypeStruct((own, bins), jnp.float32),
            in_specs=[hbm] * 6,
            out_specs=vmem,
            scratch_shapes=[
                pltpu.VMEM(sft.shape, sft.dtype),
                pltpu.VMEM(doppler.shape, doppler.dtype),
                pltpu.VMEM(antenna.shape, antenna.dtype),
                pltpu.VMEM(coarse_index.shape, coarse_index.dtype),
                pltpu.VMEM(freq_offset.shape, freq_offset.dtype),
                pltpu.SMEM(wing_width.shape, wing_width.dtype),
                pltpu.VMEM((ROWS * segs_here, doppler.shape[1]), jnp.float32),
                pltpu.VMEM((LANES, fine), jnp.float32),
                pltpu.VMEM((fine, LANES), jnp.float32),
                pltpu.VMEM((n_seg, lines, bins), jnp.float32),
                pltpu.VMEM((n_seg, 2, lines, LANES), jnp.float32),
                pltpu.VMEM((n_seg - 1, own, LANES), jnp.float32),
                pltpu.SemaphoreType.DMA((6,)),
                pltpu.SemaphoreType.DMA((n_seg - 1,)),
                pltpu.SemaphoreType.DMA((n_seg - 1,)),
                pltpu.SemaphoreType.DMA((2, n_seg)),
                pltpu.SemaphoreType.DMA((2, n_seg)),
                pltpu.SemaphoreType.DMA((n_seg - 1,)),
                pltpu.SemaphoreType.DMA((n_seg - 1,)),
            ],
            compiler_params=pltpu.CompilerParams(
                collective_id=0, has_side_effects=True, vmem_limit_bytes=40 * 1024 * 1024
            ),
        )(*operands)

    return jax.shard_map(
        per_device, mesh=mesh, in_specs=placed, out_specs=P("seg", "band"), check_vma=False
    )
```

```python
import functools
import math

import jax
import jax.numpy as jnp
from jax import lax
from jax.experimental import pallas as pl
from jax.experimental.pallas import tpu as pltpu
from jax.sharding import PartitionSpec as P

WMAX = 32
OMAX = 32
LANES = 128
ROWS = 8
MESH = pl.DeviceIdType.MESH


def half_turn(x):
    rest = x - jnp.round(x)
    angle = rest * math.pi
    square = angle * angle
    sine = jnp.zeros_like(x)
    cosine = jnp.zeros_like(x)
    for power in range(7, -1, -1):
        sign = -1.0 if power % 2 else 1.0
        cosine = cosine * square + sign / math.factorial(2 * power)
        sine = sine * square + sign / math.factorial(2 * power + 1)
    return sine * angle, cosine


def gathered_rows(rows, indices):
    first = rows.astype(jnp.bfloat16).astype(jnp.float32)
    rest = rows - first
    second = rest.astype(jnp.bfloat16).astype(jnp.float32)
    third = rest - second
    parts = jnp.concatenate([first, second, third, jnp.zeros_like(first)], axis=0)
    places = lax.broadcasted_iota(jnp.int32, (rows.shape[1], indices.shape[1]), 0)
    chosen = jnp.where(places == indices, 1.0, 0.0).astype(jnp.bfloat16)
    picked = jnp.dot(parts.astype(jnp.bfloat16), chosen, preferred_element_type=jnp.float32)
    count = rows.shape[0]
    return picked[:count] + picked[count : 2 * count] + picked[2 * count : 3 * count]


def kernel(
    n_seg,
    n_band,
    scale,
    sft_hbm,
    doppler_hbm,
    antenna_hbm,
    index_hbm,
    offset_hbm,
    wing_hbm,
    out_ref,
    sft_ref,
    doppler_ref,
    antenna_ref,
    index_ref,
    offset_ref,
    wing_ref,
    param_ref,
    fine_ref,
    column_ref,
    x_ref,
    edge_ref,
    block_ref,
    load_sem,
    x_send,
    x_recv,
    edge_send,
    edge_recv,
    block_send,
    block_recv,
):
    seg = lax.axis_index("seg")
    band = lax.axis_index("band")
    segs_here, dets, _, bins = sft_ref.shape
    fine = index_ref.shape[1]
    own = fine // n_seg
    lines = 2 * dets
    has_up = band < n_band - 1
    has_down = band > 0
    up = jnp.minimum(band + 1, n_band - 1)
    down = jnp.maximum(band - 1, 0)
    peers = [lax.rem(seg + step, n_seg) for step in range(n_seg)]

    barrier = pltpu.get_barrier_semaphore()

    def greet(peer, there):
        pl.semaphore_signal(
            barrier, inc=1, device_id={"seg": peer, "band": there}, device_id_type=MESH
        )

    for peer in peers[1:]:
        greet(peer, band)
    for there, neighbour in ((has_up, up), (has_down, down)):

        @pl.when(there)
        def _():
            for peer in peers:
                greet(peer, neighbour)

    loads = []
    for source, target in (
        (sft_hbm, sft_ref),
        (doppler_hbm, doppler_ref),
        (antenna_hbm, antenna_ref),
        (index_hbm, index_ref),
        (offset_hbm, offset_ref),
        (wing_hbm, wing_ref),
    ):
        loads.append(pltpu.make_async_copy(source, target, load_sem.at[len(loads)]))
        loads[-1].start()
    loads[0].wait()
    for s in range(segs_here):
        for d in range(dets):
            first = s * lines + 2 * d
            x_ref[0, first : first + 2, :] = sft_ref[s, d].astype(jnp.float32)
    for load in loads[1:]:
        load.wait()
    param_ref[...] = jnp.zeros_like(param_ref)
    fine_ref[...] = jnp.zeros_like(fine_ref)
    for s in range(segs_here):
        param_ref[ROWS * s : ROWS * s + 1, :] = doppler_ref[s : s + 1, :]
        for q in range(2):
            first = ROWS * s + 1 + dets * q
            param_ref[first : first + dets, :] = antenna_ref[s, q]
    for s in range(segs_here):
        rows = gathered_rows(param_ref[ROWS * s : ROWS * (s + 1), :], index_ref[s : s + 1, :])
        fine_ref[ROWS * s : ROWS * (s + 1), :] = rows
        sine, cosine = half_turn(rows[0:1])
        fine_ref[ROWS * s + 5 : ROWS * s + 6, :] = offset_ref[s : s + 1, :].astype(jnp.float32)
        fine_ref[ROWS * s + 6 : ROWS * s + 7, :] = sine
        fine_ref[ROWS * s + 7 : ROWS * s + 8, :] = cosine
    column_ref[...] = jnp.transpose(fine_ref[...])
    sides = has_up.astype(jnp.int32) + has_down.astype(jnp.int32)
    pl.semaphore_wait(barrier, n_seg - 1 + n_seg * sides)

    def edge_copy(side, step):
        start, neighbour = ((bins - LANES, up), (0, down))[side]
        return pltpu.make_async_remote_copy(
            src_ref=x_ref.at[0, :, pl.ds(start, LANES)],
            dst_ref=edge_ref.at[step, side],
            send_sem=edge_send.at[side, step],
            recv_sem=edge_recv.at[side, step],
            device_id={"seg": peers[step], "band": neighbour},
            device_id_type=MESH,
        )

    def x_copy(step):
        return pltpu.make_async_remote_copy(
            src_ref=x_ref.at[0],
            dst_ref=x_ref.at[step],
            send_sem=x_send.at[step - 1],
            recv_sem=x_recv.at[step - 1],
            device_id={"seg": peers[step], "band": band},
            device_id_type=MESH,
        )

    def block_copy(step):
        return pltpu.make_async_remote_copy(
            src_ref=column_ref.at[pl.ds(pl.multiple_of(peers[step] * own, own), own)],
            dst_ref=block_ref.at[step - 1],
            send_sem=block_send.at[step - 1],
            recv_sem=block_recv.at[step - 1],
            device_id={"seg": peers[step], "band": band},
            device_id_type=MESH,
        )

    for side, there in enumerate((has_up, has_down)):

        @pl.when(there)
        def _():
            for step in range(n_seg):
                edge_copy(side, step).start()

    for step in range(1, n_seg):
        x_copy(step).start()

    for step in range(1, n_seg):
        block_copy(step).start()

    span = 2 * (WMAX + OMAX)
    width = bins + span
    wing_low = jnp.where(has_down, wing_ref[down], 0).astype(jnp.float32)
    wing_mid = wing_ref[band].astype(jnp.float32)
    wing_high = jnp.where(has_up, wing_ref[up], 0).astype(jnp.float32)
    lane = lax.broadcasted_iota(jnp.int32, (own, span), 1)
    reach = (span // 2 - 1 - lane).astype(jnp.float32)
    place = lax.broadcasted_iota(jnp.int32, (own, bins), 1).astype(jnp.float32)

    def demodulators(columns, s):
        column = lambda row: columns[:, ROWS * s + row : ROWS * s + row + 1]
        offset = column(5)
        tap = reach - offset
        u = tap - column(0)
        centre = u == 0.0
        envelope = jnp.where(
            centre, 1.0, -column(6) / jnp.where(centre, 1.0, math.pi * u)
        )
        real_part = envelope * column(7)
        imag_part = envelope * column(6)
        blocks = []
        for wing in (wing_mid, jnp.where(offset < 0.0, wing_low, wing_high)):
            inside = (tap >= -wing) & (tap < wing)
            real = jnp.where(inside, real_part, 0.0)
            imag = jnp.where(inside, imag_part, 0.0)
            for q in range(2):
                to_real, to_imag = [], []
                for d in range(dets):
                    weight = column(1 + dets * q + d)
                    weighted_real = (weight * real).astype(jnp.bfloat16)
                    weighted_imag = (weight * imag).astype(jnp.bfloat16)
                    to_real += [weighted_real, -weighted_imag]
                    to_imag += [weighted_imag, weighted_real]
                blocks.append(jnp.concatenate(to_real, axis=1))
                blocks.append(jnp.concatenate(to_imag, axis=1))
        return jnp.concatenate(blocks, axis=0)

    def unfold(low, middle, high):
        padded = jnp.concatenate(
            [jnp.where(has_down, low, 0.0), middle, jnp.where(has_up, high, 0.0)], axis=1
        )
        margin = LANES - WMAX - OMAX
        row_at = lax.broadcasted_iota(jnp.int32, (span, LANES), 0)
        this_tile = lax.broadcasted_iota(jnp.int32, (span, LANES), 1) <= row_at
        padded = pltpu.roll(padded, padded.shape[1] - margin, 1)[:, :width]
        spreads = []
        for line in range(segs_here * lines):
            turned = []
            for at in range(0, width, LANES):
                tile = jnp.broadcast_to(padded[line : line + 1, at : at + LANES], (span, LANES))
                turned.append(pltpu.roll(tile, LANES + 1 - span, 1, stride=1, stride_axis=0))
            chosen = [
                jnp.where(this_tile, turned[at], turned[at + 1]).astype(jnp.bfloat16)
                for at in range(bins // LANES)
            ]
            spreads.append(jnp.concatenate(chosen, axis=1))
        return [
            jnp.concatenate(spreads[s * lines : (s + 1) * lines], axis=0)
            for s in range(segs_here)
        ]

    def moved_coarse(columns, s, kernels, unfolded):
        amplitude = jnp.dot(kernels, unfolded, preferred_element_type=jnp.float32)
        power = amplitude * amplitude
        parts = [power[own * part : own * (part + 1)] for part in range(8)]
        middle = (parts[0] + parts[1]) + (parts[2] + parts[3])
        beside = (parts[4] + parts[5]) + (parts[6] + parts[7])
        there = place + columns[:, ROWS * s + 5 : ROWS * s + 6]
        return jnp.where((there >= 0.0) & (there < float(bins)), middle, beside)

    def segment_sum(columns, kernels, x_slot):
        unfolded = unfold(edge_ref[x_slot, 0], x_ref[x_slot], edge_ref[x_slot, 1])
        result = None
        for s in range(segs_here):
            term = moved_coarse(columns, s, kernels[s], unfolded[s])
            result = term if result is None else result + term
        return result

    def wait_edges(step):
        for side, there in enumerate((has_down, has_up)):

            @pl.when(there)
            def _():
                edge_copy(side, step).wait_recv()

    columns = column_ref[pl.ds(pl.multiple_of(seg * own, own), own), :]
    kernels = [demodulators(columns, s) for s in range(segs_here)]
    wait_edges(0)
    total = segment_sum(columns, kernels, 0)
    for step in range(1, n_seg):
        wait_edges(step)
        x_copy(step).wait_recv()
        block_copy(step).wait_recv()
    for step in range(1, n_seg):
        columns = block_ref[step - 1]
        kernels = [demodulators(columns, s) for s in range(segs_here)]
        total = total + segment_sum(columns, kernels, step)
    out_ref[...] = total * scale

    for step in range(1, n_seg):
        x_copy(step).wait_send()
        block_copy(step).wait_send()
    for side, there in enumerate((has_up, has_down)):

        @pl.when(there)
        def _():
            for step in range(n_seg):
                edge_copy(side, step).wait_send()


def solution(mesh):
    n_seg = mesh.shape["seg"]
    n_band = mesh.shape["band"]
    placed = (
        P("seg", None, None, "band"),
        P("seg", None),
        P("seg", None, None, None),
        P("seg", None),
        P("seg", None),
        P(),
    )

    def per_device(sft, doppler, antenna, coarse_index, freq_offset, wing_width):
        segs_here, dets, _, bins = sft.shape
        fine = coarse_index.shape[1]
        own = fine // n_seg
        lines = segs_here * dets * 2
        operands = [
            pltpu.with_memory_space_constraint(operand, pltpu.HBM)
            for operand in (sft, doppler, antenna, coarse_index, freq_offset, wing_width)
        ]
        vmem = pl.BlockSpec(memory_space=pltpu.VMEM)
        hbm = pl.BlockSpec(memory_space=pltpu.HBM)
        return pl.pallas_call(
            functools.partial(kernel, n_seg, n_band, 0.25 / (segs_here * n_seg)),
            out_shape=jax.ShapeDtypeStruct((own, bins), jnp.float32),
            in_specs=[hbm] * 6,
            out_specs=vmem,
            scratch_shapes=[
                pltpu.VMEM(sft.shape, sft.dtype),
                pltpu.VMEM(doppler.shape, doppler.dtype),
                pltpu.VMEM(antenna.shape, antenna.dtype),
                pltpu.VMEM(coarse_index.shape, coarse_index.dtype),
                pltpu.VMEM(freq_offset.shape, freq_offset.dtype),
                pltpu.SMEM(wing_width.shape, wing_width.dtype),
                pltpu.VMEM((ROWS * segs_here, doppler.shape[1]), jnp.float32),
                pltpu.VMEM((LANES, fine), jnp.float32),
                pltpu.VMEM((fine, LANES), jnp.float32),
                pltpu.VMEM((n_seg, lines, bins), jnp.float32),
                pltpu.VMEM((n_seg, 2, lines, LANES), jnp.float32),
                pltpu.VMEM((n_seg - 1, own, LANES), jnp.float32),
                pltpu.SemaphoreType.DMA((6,)),
                pltpu.SemaphoreType.DMA((n_seg - 1,)),
                pltpu.SemaphoreType.DMA((n_seg - 1,)),
                pltpu.SemaphoreType.DMA((2, n_seg)),
                pltpu.SemaphoreType.DMA((2, n_seg)),
                pltpu.SemaphoreType.DMA((n_seg - 1,)),
                pltpu.SemaphoreType.DMA((n_seg - 1,)),
            ],
            compiler_params=pltpu.CompilerParams(
                collective_id=0, has_side_effects=True, vmem_limit_bytes=40 * 1024 * 1024
            ),
        )(*operands)

    return jax.shard_map(
        per_device, mesh=mesh, in_specs=placed, out_specs=P("seg", "band"), check_vma=False
    )
```
